32 devices in a mesh: dom: 8 (over y, x, core), orient: 4 (over z).
Axes of the slice: x: 2, y: 2, z: 4, core: 2. Of those that a mesh axis runs over, the one named last changes fastest.
Arguments:
- particles: bfloat16 [64, 2, 8192], P('dom'), may hold values from -4 to 4
- references: bfloat16 [64, 2, 8192], P('orient'), may hold values from -1.7 to 1.7
- phases: float32 [16, 8192], replicated, may hold values from -3.1416 to 3.1416
- mask: int32 [64, 64], P('dom', 'orient'), may hold values from 0 to 1, as said below
- ctf_group: int32 [64], replicated, may hold values from 0 to 63
- ctf_table: float32 [64, 64], replicated, may hold values from 0.1 to 1
- shell_index: int32 [8192], replicated, may hold values from 0 to 63
- sigma2: float32 [64], replicated, may hold values from 8 to 32
Outputs:
- posterior: float32 [64, 16, 64], P('dom', None, 'orient')
- image_sums: float32 [64, 2, 8192], P('orient', None, 'dom')
- ctf_weights: float32 [64, 64], P('orient')
- shell_noise: float32 [64], replicated
The draws below stay inside these ranges and needn't reach their ends.
Inputs may be any that keep to these rules, and one draw needn't show every extreme that they name: `mask`: every particle allows at least one orientation.
All inputs are finite; a program needn't handle non-finite values.
Results may differ from the reference program's by a relative error of at most 0.0041.
Values may be sent and summed in bfloat16 or wider, within the bound.
No kernel may reach another device: no remote copies, remote signals or barrier semaphores. Data moves between devices by JAX's collectives and lax.ppermute only.
A program may use at most 192 MiB of HBM per device.

```python
import math
import jax
import jax.numpy as jnp
from jax import lax

PIX = 8192
SHELLS = 64
GROUPS = 64
TRANS = 16
PARTICLES = 64
ORIENTS = 64


def pairing(key):
    target = jax.random.randint(jax.random.fold_in(key, 11), (PARTICLES,), 0, ORIENTS)
    forced = jax.random.randint(jax.random.fold_in(key, 13), (), 0, PARTICLES)
    return (target, forced)


def reference_planes(key):
    spread_part = jax.random.uniform(jax.random.fold_in(key, 21), (ORIENTS, PIX), jnp.float32, -1.0, 1.0)
    angle_plane = jax.random.uniform(jax.random.fold_in(key, 22), (ORIENTS, PIX), jnp.float32, -3.14159, 3.14159)
    amplitude = jnp.sqrt(2.0 * (1.0 + 0.4 * spread_part))
    return jnp.stack([amplitude * jnp.cos(angle_plane), amplitude * jnp.sin(angle_plane)], axis=1)


def phase_table(key):
    return jax.random.uniform(jax.random.fold_in(key, 31), (TRANS, PIX), jnp.float32, -3.14159, 3.14159)


def draw_references(key, part):
    return reference_planes(key).astype(jnp.bfloat16)


def draw_phases(key, part):
    return phase_table(key)


def draw_mask(key, part):
    target, forced = pairing(key)
    level_rows = jax.random.randint(jax.random.fold_in(key, 51), (PARTICLES, 1), 1, 5)
    roll_table = jax.random.randint(jax.random.fold_in(key, 52), (PARTICLES, ORIENTS), 0, 8)
    columns = jnp.arange(ORIENTS, dtype=jnp.int32)[None, :]
    allowed = (roll_table < level_rows) | (columns == target[:, None])
    return allowed.astype(jnp.int32)


def draw_particles(key, part):
    target, forced = pairing(key)
    planes = reference_planes(key)[target]
    angle_row = phase_table(key)[0]
    cosine = jnp.cos(angle_row)
    sine_part = jnp.sin(angle_row)
    real_part = planes[:, 0] * cosine + planes[:, 1] * sine_part
    imag_part = planes[:, 1] * cosine - planes[:, 0] * sine_part
    aligned = jnp.stack([real_part, imag_part], axis=1)
    level_rows = jax.random.randint(jax.random.fold_in(key, 43), (PARTICLES, 1, 1), 1, 4).astype(jnp.float32)
    strength = 0.4 + 0.2 * level_rows
    faint_level = 0.002 * (level_rows - 1.0)
    indices = jnp.arange(PARTICLES, dtype=jnp.int32)
    noise_part = jax.random.truncated_normal(jax.random.fold_in(key, 41), -6.0, 6.0, (PARTICLES, 2, PIX), jnp.float32)
    is_aligned = (indices == forced)[:, None, None]
    row_scale = jax.random.uniform(jax.random.fold_in(key, 42), (PARTICLES, 1, 1), jnp.float32, 0.15, 0.3)
    values = jnp.where(is_aligned, strength * aligned + 0.3 * noise_part, faint_level * aligned + row_scale * noise_part)
    return values.astype(jnp.bfloat16)


def place_ends(result, own_key, low, high):
    longest = result.shape.index(max(result.shape))
    spots = []
    for shift in (0, 1):
        where = [jax.random.randint(jax.random.fold_in(own_key, axis), (), 0, length) for axis, length in enumerate(result.shape)]
        where[longest] = (where[longest] + shift) % result.shape[longest]
        spots.append(tuple(where))
    return result.at[spots[0]].set(low).at[spots[1]].set(high)


def setup_inputs(seed: int = 0) -> dict:
    seeds = jax.random.split(jax.random.key(seed), 9)
    particles = draw_particles(jax.random.fold_in(seeds[8], 71), 0)
    references = draw_references(jax.random.fold_in(seeds[8], 71), 0)
    phases = draw_phases(jax.random.fold_in(seeds[8], 71), 0)
    mask = draw_mask(jax.random.fold_in(seeds[8], 71), 0)
    ctf_group = place_ends(jax.random.randint(seeds[4], (PARTICLES,), 0, GROUPS), jax.random.fold_in(seeds[4], 1), 0, GROUPS - 1).astype(jnp.int32)
    ctf_table = jnp.clip(jax.random.uniform(seeds[5], (GROUPS, SHELLS), jnp.float32, 0.1, 1.0), 0.1, 1.0)
    shell_index = place_ends(jax.random.randint(seeds[6], (PIX,), 0, SHELLS), jax.random.fold_in(seeds[6], 1), 0, SHELLS - 1).astype(jnp.int32)
    sigma2 = jnp.clip(jnp.exp(jax.random.uniform(seeds[7], (SHELLS,), jnp.float32, math.log(8.0), math.log(32.0))), 8.0, 32.0)
    return {"particles": particles, "references": references, "phases": phases, "mask": mask, "ctf_group": ctf_group, "ctf_table": ctf_table, "shell_index": shell_index, "sigma2": sigma2}


def shell_sum(values, shell_index):
    moved = jnp.moveaxis(values, -1, 0)
    summed = jax.ops.segment_sum(moved, shell_index, num_segments=SHELLS)
    return jnp.moveaxis(summed, 0, -1)


def make_image(planes, ctf_pix, angle_row):
    cosine = jnp.cos(angle_row)
    sine_part = jnp.sin(angle_row)
    real_part = planes[:, 0]
    imag_part = planes[:, 1]
    shifted = jnp.stack([real_part * cosine - imag_part * sine_part, real_part * sine_part + imag_part * cosine], axis=1)
    rounded = lax.optimization_barrier((ctf_pix[:, None, :] * shifted).astype(jnp.bfloat16))
    return rounded.astype(jnp.float32)


def reference(particles, references, phases, mask, ctf_group, ctf_table, shell_index, sigma2):
    highest = lax.Precision.HIGHEST
    ctf_rows = ctf_table[ctf_group]
    ctf_pix = ctf_rows[:, shell_index]
    sigma_pix = sigma2[shell_index]
    refs_wide = references.astype(jnp.float32)
    weighted = lax.optimization_barrier((refs_wide / sigma_pix).astype(jnp.bfloat16)).astype(jnp.float32)
    ref_norm = shell_sum(jnp.sum(refs_wide * refs_wide, axis=1), shell_index)
    energy = ref_norm / sigma2
    ctf_square = ctf_rows * ctf_rows
    quadratic = 0.5 * jnp.dot(ctf_square, energy.T, precision=highest)
    planes = particles.astype(jnp.float32)

    def score_one(index):
        images = make_image(planes, ctf_pix, phases[index])
        return jnp.einsum("pcx,ocx->po", images, weighted, precision=highest) - quadratic

    stacked = lax.map(score_one, jnp.arange(TRANS))
    scores = jnp.transpose(stacked, (1, 0, 2))
    scores = jnp.where((mask == 1)[:, None, :], scores, -1e30)
    peak = jnp.max(scores, axis=(1, 2), keepdims=True)
    exponent = jnp.exp(scores - peak)
    posterior = exponent / jnp.sum(exponent, axis=(1, 2), keepdims=True)
    post_wide = lax.optimization_barrier(posterior.astype(jnp.bfloat16)).astype(jnp.float32)

    def add_block(running, index):
        images = make_image(planes, ctf_pix, phases[index])
        return running + jnp.einsum("po,pcx->ocx", post_wide[:, index, :], images, precision=highest), None

    image_sums, unused = lax.scan(add_block, jnp.zeros((ORIENTS, 2, PIX), jnp.float32), jnp.arange(TRANS))
    ctf_weights = jnp.dot(jnp.sum(posterior, axis=1).T, ctf_square, precision=highest)
    part_norm = shell_sum(jnp.sum(planes * planes, axis=1), shell_index)
    term_one = jnp.sum(part_norm * jnp.sum(posterior, axis=(1, 2))[:, None], axis=0)
    term_two = -2.0 * shell_sum(jnp.sum(image_sums * refs_wide, axis=(0, 1)), shell_index)
    term_three = jnp.sum(ctf_weights * ref_norm, axis=0)
    shell_noise = (term_one + term_two + term_three) / (PARTICLES * PIX / SHELLS)
    return (posterior, image_sums, ctf_weights, shell_noise)
```

```python
import functools

import jax
import jax.numpy as jnp
from jax import lax
from jax.experimental import pallas as pl
from jax.experimental.pallas import tpu as pltpu
from jax.sharding import PartitionSpec as P

f32 = jnp.float32
bf16 = jnp.bfloat16
highest = lax.Precision.HIGHEST
vmem_bytes = 48 * 1024 * 1024
lanes = 128
stat_rows = 8

sin_terms = (0.9999999765, -0.1666664763, 0.008332899647, -0.0001980088726, 2.590467298e-06)
cos_terms = (0.9999999998, -0.4999999942, 0.04166663615, -0.001388836116, 2.476015062e-05, -2.605130164e-07)


def horner(terms, z):
    total = jnp.full_like(z, terms[-1])
    for term in terms[-2::-1]:
        total = total * z + term
    return total


def sin_cos(angle):
    half = angle * 0.5
    z = half * half
    s = half * horner(sin_terms, z)
    c = horner(cos_terms, z)
    twice = s + s
    return twice * c, 1.0 - twice * s


def pieces(x, count):
    out = []
    rest = x
    for step in range(count):
        piece = rest.astype(bf16)
        out.append(piece)
        if step + 1 < count:
            rest = rest - piece.astype(f32)
    return out


def nt(a, b, **kw):
    return lax.dot_general(a, b, (((1,), (1,)), ((), ())), preferred_element_type=f32, **kw)


def tn(a, b, **kw):
    return lax.dot_general(a, b, (((0,), (0,)), ((), ())), preferred_element_type=f32, **kw)


def nn(a, b, **kw):
    return lax.dot_general(a, b, (((1,), (0,)), ((), ())), preferred_element_type=f32, **kw)


def one_hot(index_row, shells):
    rows = lax.broadcasted_iota(jnp.int32, (shells, index_row.shape[1]), 0)
    return jnp.where(rows == index_row, 1.0, 0.0).astype(bf16)


def write_images(img_ref, row0, col0, scaled_r, scaled_m, cosine, sine):
    trans, width = cosine.shape
    for i in range(scaled_r.shape[0]):
        r = jnp.broadcast_to(scaled_r[i : i + 1], (trans, width))
        m = jnp.broadcast_to(scaled_m[i : i + 1], (trans, width))
        rows = pl.ds(row0 + i * trans, trans)
        img_ref[0, rows, pl.ds(col0, width)] = (r * cosine - m * sine).astype(bf16)
        img_ref[1, rows, pl.ds(col0, width)] = (r * sine + m * cosine).astype(bf16)


def score_kernel(
    chunk,
    group_ref,
    part_ref,
    refs_ref,
    phase_ref,
    shell_ref,
    mask_ref,
    table_ref,
    sigma_ref,
    send_ref,
    stat_ref,
    e_ref,
    img_ref,
    planes_ref,
    hot_ref,
    rows_ref,
    norm_ref,
    score_ref,
):
    part_dev, _, pixels = part_ref.shape
    ori_dev = refs_ref.shape[0]
    trans = phase_ref.shape[0]
    shells = table_ref.shape[1]
    dests, _, _, width = send_ref.shape
    pairs = part_dev * trans
    blocks = pixels // chunk
    first = lax.axis_index("dom") * part_dev

    for i in range(part_dev):
        rows_ref[pl.ds(i, 1), :] = table_ref[pl.ds(group_ref[first + i], 1), :]
    ctf_rows = rows_ref[...]
    sigma = sigma_ref[...]
    inverse = jnp.broadcast_to(1.0 / sigma, (8, shells))
    table = jnp.concatenate(
        [p.astype(f32) for p in pieces(ctf_rows, 3)] + [p.astype(f32) for p in pieces(inverse, 3)], axis=0
    ).astype(bf16)
    score_ref[...] = jnp.zeros_like(score_ref)
    norm_ref[...] = jnp.zeros_like(norm_ref)

    def first_pass(step, carry):
        col0 = pl.multiple_of(step * chunk, chunk)
        cols = pl.ds(col0, chunk)
        hot = one_hot(shell_ref[:, cols], shells)
        hot_ref[:, cols] = hot
        picked = nn(table, hot)
        n = part_dev
        ctf_pix = picked[0:n] + picked[n : 2 * n] + picked[2 * n : 3 * n]
        inv_sigma = picked[3 * n : 3 * n + 1] + picked[3 * n + 8 : 3 * n + 9] + picked[3 * n + 16 : 3 * n + 17]
        part = part_ref[:, :, cols].astype(f32)
        part_r = part[:, 0, :]
        part_m = part[:, 1, :]
        refs = refs_ref[:, :, cols].astype(f32)
        refs_r = refs[:, 0, :]
        refs_m = refs[:, 1, :]
        planes_ref[0, :, cols] = refs_r.astype(bf16)
        planes_ref[1, :, cols] = refs_m.astype(bf16)
        squares = pieces(refs_r * refs_r + refs_m * refs_m, 2) + pieces(part_r * part_r + part_m * part_m, 2)
        for k, offset in enumerate((0, ori_dev, 2 * ori_dev, 2 * ori_dev + part_dev)):
            size = squares[k].shape[0]
            norm_ref[pl.ds(offset, size), :] += nt(squares[k], hot)
        sine, cosine = sin_cos(phase_ref[:, cols])
        write_images(img_ref, 0, col0, part_r * ctf_pix, part_m * ctf_pix, cosine, sine)
        score_ref[...] += nt((refs_r * inv_sigma).astype(bf16), img_ref[0, :, cols]) + nt(
            (refs_m * inv_sigma).astype(bf16), img_ref[1, :, cols]
        )
        return carry

    lax.fori_loop(0, blocks, first_pass, 0)

    ref_norm = norm_ref[0:ori_dev, :] + norm_ref[ori_dev : 2 * ori_dev, :]
    part_norm = norm_ref[2 * ori_dev : 2 * ori_dev + part_dev, :] + norm_ref[2 * ori_dev + part_dev :, :]
    ctf_square = ctf_rows * ctf_rows
    square_wide = jnp.broadcast_to(ctf_square[:, None, :], (part_dev, trans, shells)).reshape(pairs, shells)
    energy = ref_norm / sigma
    quadratic = 0.5 * nt(energy, square_wide, precision=highest)
    lane_part = lax.broadcasted_iota(jnp.int32, (part_dev, pairs), 1) // trans
    own = lane_part == lax.broadcasted_iota(jnp.int32, (part_dev, pairs), 0)
    own_wide = jnp.where(own, 1.0, 0.0)
    mask_wide = tn(mask_ref[...].astype(f32), own_wide)
    scores = jnp.where(mask_wide > 0.5, score_ref[...] - quadratic, -1e30)
    top = jnp.max(scores, axis=0, keepdims=True)
    peak = jnp.max(jnp.where(own, jnp.broadcast_to(top, own.shape), -3e38), axis=1, keepdims=True)
    peak_lane = jnp.max(jnp.where(own, jnp.broadcast_to(peak, own.shape), -3e38), axis=0, keepdims=True)
    e = jnp.exp(scores - peak_lane)
    e_ref[...] = e
    total = jnp.sum(
        jnp.where(own, jnp.broadcast_to(jnp.sum(e, axis=0, keepdims=True), own.shape), 0.0), axis=1, keepdims=True
    )

    e_pieces = pieces(e, 2)
    per_row = width // lanes
    for dest in range(dests):
        send_ref[dest, 0:part_dev] = part_ref[:, :, dest * width : (dest + 1) * width]
    half = ori_dev // 2
    for k in range(2):
        piece = e_pieces[k].astype(f32)
        for c in range(half):
            q = k * half + c
            tile = jnp.concatenate([piece[c : c + 1], piece[half + c : half + c + 1]], axis=0).astype(bf16)
            for dest in range(dests):
                send_ref[dest, part_dev + q // per_row, :, (q % per_row) * lanes : (q % per_row + 1) * lanes] = tile

    e_rows = jnp.concatenate([p.astype(f32) for p in e_pieces], axis=0).T.astype(bf16)

    def second_pass(step, carry):
        cols = pl.ds(pl.multiple_of(step * chunk, chunk), chunk)
        wide = jnp.zeros((pairs, chunk), f32)
        for p in range(2):
            plane = planes_ref[p, :, cols]
            mixed = nn(e_rows, jnp.concatenate([plane, plane], axis=0))
            wide = wide + mixed * img_ref[p, :, cols].astype(f32)
        folded = wide.reshape(part_dev, trans // 8, 8, chunk).sum(axis=1).reshape(part_dev * 8, chunk)
        hot = hot_ref[:, cols]
        high, low = pieces(folded, 2)
        return carry + nt(high, hot) + nt(low, hot)

    cross = lax.fori_loop(0, blocks, second_pass, jnp.zeros((part_dev * 8, shells), f32))
    cross = cross.reshape(part_dev, 8, shells).sum(axis=1)
    orient_sums = nt(own_wide, e, precision=highest)
    third = ctf_square * nn(orient_sums, ref_norm, precision=highest)
    noise = part_norm * total - 2.0 * cross + third
    fill = (part_dev, (lanes - shells) // 2)
    stat = jnp.concatenate([noise, jnp.broadcast_to(peak, fill), jnp.broadcast_to(total, fill)], axis=1)
    for dest in range(stat_ref.shape[0]):
        stat_ref[dest] = stat


def column_kernel(
    group_ref,
    recv_ref,
    phase_hbm,
    shell_hbm,
    table_ref,
    img_ref,
    phase_ref,
    shell_ref,
    rows_ref,
    sems,
):
    sources, _, _, width = recv_ref.shape
    part_dev = stat_rows
    trans = phase_ref.shape[0]
    shells = table_ref.shape[1]
    start = pl.multiple_of(lax.axis_index("dom") * width, width)
    phase_copy = pltpu.make_async_copy(phase_hbm.at[:, pl.ds(start, width)], phase_ref, sems.at[0])
    shell_copy = pltpu.make_async_copy(shell_hbm.at[:, pl.ds(start, width)], shell_ref, sems.at[1])
    phase_copy.start()
    shell_copy.start()
    for i in range(sources * part_dev):
        rows_ref[pl.ds(i, 1), :] = table_ref[pl.ds(group_ref[i], 1), :]
    shell_copy.wait()
    phase_copy.wait()
    hot = one_hot(shell_ref[...], shells)
    sine, cosine = sin_cos(phase_ref[...])

    def source_step(src, carry):
        rows = pl.ds(pl.multiple_of(src * part_dev, part_dev), part_dev)
        ctf_pix = sum(nn(p, hot) for p in pieces(rows_ref[rows, :], 3))
        part = recv_ref[src, 0:part_dev].astype(f32)
        row0 = pl.multiple_of(src * part_dev * trans, part_dev * trans)
        write_images(img_ref, row0, 0, part[:, 0, :] * ctf_pix, part[:, 1, :] * ctf_pix, cosine, sine)
        return carry

    lax.fori_loop(0, sources, source_step, 0)


def sum_kernel(
    orients,
    scale,
    group_ref,
    img_ref,
    recv_ref,
    stat_ref,
    e_ref,
    table_ref,
    post_ref,
    sums_ref,
    weights_ref,
    noise_ref,
    half_ref,
    rows_ref,
):
    sources, _, _, width = recv_ref.shape
    part_dev = stat_rows
    ori_dev, pairs = e_ref.shape
    trans = pairs // part_dev
    shells = table_ref.shape[1]
    fill = (lanes - shells) // 2
    me = lax.axis_index("dom")
    mine = lax.axis_index("orient")
    for i in range(sources * part_dev):
        rows_ref[pl.ds(i, 1), :] = table_ref[pl.ds(group_ref[i], 1), :]
    lane_part = lax.broadcasted_iota(jnp.int32, (part_dev, pairs), 1) // trans
    own = lane_part == lax.broadcasted_iota(jnp.int32, (part_dev, pairs), 0)
    per_row = width // lanes
    half = ori_dev // 2

    def factors(src):
        stats = [stat_ref[src * orients + o] for o in range(orients)]
        peaks = [s[:, shells : shells + 1] for s in stats]
        totals = [s[:, shells + fill : shells + fill + 1] for s in stats]
        peak = functools.reduce(jnp.maximum, peaks)
        shares = [jnp.exp(p - peak) for p in peaks]
        total = sum(s * t for s, t in zip(shares, totals))
        inverse = 1.0 / total
        noise = sum(share * stat[:, 0:shells] for share, stat in zip(shares, stats)) * inverse
        my_peak = stat_ref[src * orients + mine][:, shells : shells + 1]
        factor = jnp.exp(my_peak - peak) * inverse
        lane = jnp.sum(jnp.where(own, jnp.broadcast_to(factor, own.shape), 0.0), axis=0, keepdims=True)
        return noise, lane

    def source_step(src, carry):
        noise, weights = carry
        part_noise, lane = factors(src)
        tiles = []
        for k in range(2):
            tops, bottoms = [], []
            for c in range(half):
                q = k * half + c
                col = (q % per_row) * lanes
                tile = recv_ref[src, part_dev + q // per_row, :, col : col + lanes].astype(f32)
                tops.append(tile[0:1])
                bottoms.append(tile[1:2])
            tiles.append(jnp.concatenate(tops + bottoms, axis=0))
        post = (tiles[0] + tiles[1]) * lane
        half_ref[:, pl.ds(pl.multiple_of(src * pairs, pairs), pairs)] = post.astype(bf16)
        rows = rows_ref[pl.ds(pl.multiple_of(src * part_dev, part_dev), part_dev), :]
        per_part = nt(post, jnp.where(own, 1.0, 0.0), precision=highest)
        weights = weights + nn(per_part, rows * rows, precision=highest)
        return noise + part_noise, weights

    noise, weights = lax.fori_loop(
        0, sources, source_step, (jnp.zeros((part_dev, shells), f32), jnp.zeros((ori_dev, shells), f32))
    )
    weights_ref[...] = weights
    noise_ref[...] = jnp.sum(noise, axis=0, keepdims=True) * scale
    _, lane = factors(me)
    post_ref[...] = (e_ref[...] * lane).T
    post_half = half_ref[...]
    for p in range(2):
        sums_ref[:, p, :] = nn(post_half, img_ref[p])


def on_device(particles, references, phases, mask, ctf_group, ctf_table, shell_index, sigma2):
    part_dev, _, pixels = particles.shape
    ori_dev = references.shape[0]
    trans = phases.shape[0]
    groups, shells = ctf_table.shape
    dom = lax.axis_size("dom")
    orients = lax.axis_size("orient")
    width = pixels // dom
    pairs = part_dev * trans
    e_rows = 2 * ori_dev * pairs // (2 * width)
    chunk = 512
    shell_row = shell_index.reshape(1, pixels)
    vmem = pl.BlockSpec(memory_space=pltpu.VMEM)
    smem = pl.BlockSpec(memory_space=pltpu.SMEM)
    anywhere = pl.BlockSpec(memory_space=pl.ANY)
    params = pltpu.CompilerParams(vmem_limit_bytes=vmem_bytes)

    send, stat, e = pl.pallas_call(
        functools.partial(score_kernel, chunk),
        out_shape=(
            jax.ShapeDtypeStruct((dom, part_dev + e_rows, 2, width), bf16),
            jax.ShapeDtypeStruct((dom * orients, stat_rows, lanes), f32),
            jax.ShapeDtypeStruct((ori_dev, pairs), f32),
        ),
        in_specs=[smem] + [vmem] * 7,
        out_specs=(vmem, vmem, vmem),
        scratch_shapes=[
            pltpu.VMEM((2, pairs, pixels), bf16),
            pltpu.VMEM((2, ori_dev, pixels), bf16),
            pltpu.VMEM((shells, pixels), bf16),
            pltpu.VMEM((part_dev, shells), f32),
            pltpu.VMEM((2 * (ori_dev + part_dev), shells), f32),
            pltpu.VMEM((ori_dev, pairs), f32),
        ],
        compiler_params=params,
        name="scores",
    )(ctf_group, particles, references, phases, shell_row, mask, ctf_table, sigma2.reshape(1, shells))

    recv = lax.all_to_all(send, "dom", 0, 0)
    stats = lax.all_to_all(stat, ("dom", "orient"), 0, 0)

    images = pl.pallas_call(
        column_kernel,
        out_shape=jax.ShapeDtypeStruct((2, dom * pairs, width), bf16),
        in_specs=[smem, vmem, anywhere, anywhere, vmem],
        out_specs=vmem,
        scratch_shapes=[
            pltpu.VMEM((trans, width), f32),
            pltpu.VMEM((1, width), jnp.int32),
            pltpu.VMEM((dom * part_dev, shells), f32),
            pltpu.SemaphoreType.DMA((2,)),
        ],
        compiler_params=params,
        name="columns",
    )(ctf_group, recv, phases, shell_row, ctf_table)

    scale = shells / (part_dev * dom * pixels)
    posterior, image_sums, ctf_weights, noise = pl.pallas_call(
        functools.partial(sum_kernel, orients, scale),
        out_shape=(
            jax.ShapeDtypeStruct((pairs, ori_dev), f32),
            jax.ShapeDtypeStruct((ori_dev, 2, width), f32),
            jax.ShapeDtypeStruct((ori_dev, shells), f32),
            jax.ShapeDtypeStruct((1, shells), f32),
        ),
        in_specs=[smem] + [vmem] * 5,
        out_specs=(vmem, vmem, vmem, vmem),
        scratch_shapes=[
            pltpu.VMEM((ori_dev, dom * pairs), bf16),
            pltpu.VMEM((dom * part_dev, shells), f32),
        ],
        compiler_params=params,
        name="sums",
    )(ctf_group, images, recv, stats, e, ctf_table)
    return (
        posterior.reshape(part_dev, trans, ori_dev),
        image_sums,
        ctf_weights,
        noise.reshape(shells),
    )


def solution(mesh):
    return jax.shard_map(
        on_device,
        mesh=mesh,
        in_specs=(
            P("dom", None, None),
            P("orient", None, None),
            P(),
            P("dom", "orient"),
            P(),
            P(),
            P(),
            P(),
        ),
        out_specs=(P("dom", None, "orient"), P("orient", None, "dom"), P("orient", None), P()),
        check_vma=False,
    )
```

```python
import functools

import jax
import jax.numpy as jnp
from jax import lax
from jax.experimental import pallas as pl
from jax.experimental.pallas import tpu as pltpu
from jax.sharding import PartitionSpec as P

f32 = jnp.float32
bf16 = jnp.bfloat16
highest = lax.Precision.HIGHEST
vmem_bytes = 60 * 1024 * 1024
lanes = 128

sin_terms = (0.9999999766, -0.1666664762, 0.008332899654, -0.000198008873, 2.590467297e-06)
cos_terms = (0.9999999998, -0.4999999936, 0.04166663624, -0.001388836119, 2.47601506e-05, -2.605130157e-07)


def horner(terms, z):
    total = terms[-1] * z + terms[-2]
    for term in terms[-3::-1]:
        total = total * z + term
    return total


def sin_cos(angle):
    half = angle * 0.5
    z = half * half
    s = half * horner(sin_terms, z)
    c = horner(cos_terms, z)
    twice = s + s
    return twice * c, 1.0 - twice * s


def pieces(x, count):
    out = []
    rest = x
    for step in range(count):
        piece = rest.astype(bf16)
        out.append(piece)
        if step + 1 < count:
            rest = rest - piece.astype(f32)
    return out


def nt(a, b, **kw):
    return lax.dot_general(a, b, (((1,), (1,)), ((), ())), preferred_element_type=f32, **kw)


def tn(a, b, **kw):
    return lax.dot_general(a, b, (((0,), (0,)), ((), ())), preferred_element_type=f32, **kw)


def nn(a, b, **kw):
    return lax.dot_general(a, b, (((1,), (0,)), ((), ())), preferred_element_type=f32, **kw)


def one_hot(index_row, shells):
    rows = lax.broadcasted_iota(jnp.int32, (shells, index_row.shape[1]), 0)
    return jnp.where(rows == index_row, 1.0, 0.0).astype(bf16)


def start_all(pairs, sems):
    copies = [pltpu.make_async_copy(src, dst, sems.at[k]) for k, (src, dst) in enumerate(pairs)]
    for copy in copies:
        copy.start()
    return copies


def split_planes(src, dst_ref, row0):
    items, tiles, load = src
    for tile in range(tiles):
        for item in range(items):
            dst_ref[pl.ds(row0 + (tile * items + item) * 2, 2), :] = load(item, tile).astype(f32)


def read_plane(ref, row0, items, tile, plane):
    return ref[pl.ds(row0 + tile * items * 2 + plane, items, 2), :]


def write_images(store, scaled_ref, scaled_col, cosine, sine, count):
    trans = cosine.shape[0]
    cols = pl.ds(scaled_col, lanes)
    for i in range(count):
        r = jnp.broadcast_to(scaled_ref[i : i + 1, cols], (trans, lanes))
        m = jnp.broadcast_to(scaled_ref[count + i : count + i + 1, cols], (trans, lanes))
        store(0, i, (r * cosine - m * sine).astype(bf16))
        store(1, i, (r * sine + m * cosine).astype(bf16))


def pack_kernel(part_hbm, out_hbm, held_ref, in_sems, out_sems):
    dests, _, _, width = out_hbm.shape
    loads = [
        pltpu.make_async_copy(part_hbm.at[:, :, pl.ds(dest * width, width)], held_ref.at[dest], in_sems.at[dest])
        for dest in range(dests)
    ]
    for load in loads:
        load.start()
    stores = []
    for dest in range(dests):
        loads[dest].wait()
        stores.append(pltpu.make_async_copy(held_ref.at[dest], out_hbm.at[dest], out_sems.at[dest]))
        stores[dest].start()
    for store in stores:
        store.wait()


def score_kernel(
    chunk,
    groups,
    group_ref,
    part_hbm,
    refs_hbm,
    phase_hbm,
    shell_hbm,
    mask_hbm,
    table_hbm,
    sigma_hbm,
    message_ref,
    e_ref,
    part_ref,
    refs_ref,
    phase_ref,
    shell_ref,
    mask_ref,
    table_ref,
    sigma_ref,
    part_rows,
    refs_rows,
    img_ref,
    planes_ref,
    hot_ref,
    scaled_ref,
    rows_ref,
    small_sems,
    big_sems,
):
    part_dev, _, pixels = part_ref.shape
    ori_dev = refs_ref.shape[0]
    trans = phase_ref.shape[0]
    shells = table_ref.shape[1]
    pairs = part_dev * trans
    blocks = pixels // chunk
    tiles = chunk // lanes
    first = lax.axis_index("dom") * part_dev
    small = start_all([(table_hbm, table_ref), (sigma_hbm, sigma_ref), (shell_hbm, shell_ref), (mask_hbm, mask_ref)], small_sems)
    big = []
    for g in range(groups):
        cols = pl.ds(g * (pixels // groups), pixels // groups)
        big.append(
            start_all(
                [
                    (part_hbm.at[:, :, cols], part_ref.at[:, :, cols]),
                    (phase_hbm.at[:, cols], phase_ref.at[:, cols]),
                    (refs_hbm.at[:, :, cols], refs_ref.at[:, :, cols]),
                ],
                big_sems.at[g],
            )
        )
    for copy in small:
        copy.wait()

    for i in range(part_dev):
        rows_ref[pl.ds(i, 1), :] = table_ref[pl.ds(group_ref[first + i], 1), :]
    ctf_rows = rows_ref[...]
    sigma = sigma_ref[...]
    inverse = jnp.broadcast_to(1.0 / sigma, (8, shells))
    table = jnp.concatenate(
        [p.astype(f32) for p in pieces(ctf_rows, 3)] + [p.astype(f32) for p in pieces(inverse, 3)], axis=0
    ).astype(bf16)
    n = part_dev
    norms = None
    scores = None
    for step in range(blocks):
        if step % (blocks // groups) == 0:
            for copy in big[step // (blocks // groups)]:
                copy.wait()
        col0 = step * chunk
        cols = pl.ds(col0, chunk)
        hot = one_hot(shell_ref[:, cols], shells)
        hot_ref[:, cols] = hot
        picked = nn(table, hot)
        ctf_pix = picked[0:n] + picked[n : 2 * n] + picked[2 * n : 3 * n]
        inv_sigma = picked[3 * n : 3 * n + 8] + picked[3 * n + 8 : 3 * n + 16] + picked[3 * n + 16 : 3 * n + 24]
        part0 = step * tiles * part_dev * 2
        refs0 = step * tiles * ori_dev * 2
        split_planes((part_dev, tiles, lambda i, t: part_ref[i, :, pl.ds(col0 + t * lanes, lanes)]), part_rows, part0)
        split_planes((ori_dev, tiles, lambda j, t: refs_ref[j, :, pl.ds(col0 + t * lanes, lanes)]), refs_rows, refs0)
        squares = []
        weighted = [[], []]
        for t in range(tiles):
            here = slice(t * lanes, (t + 1) * lanes)
            tcols = pl.ds(col0 + t * lanes, lanes)
            part_r = read_plane(part_rows, part0, part_dev, t, 0)
            part_m = read_plane(part_rows, part0, part_dev, t, 1)
            refs_r = read_plane(refs_rows, refs0, ori_dev, t, 0)
            refs_m = read_plane(refs_rows, refs0, ori_dev, t, 1)
            ctf = ctf_pix[:, here]
            scaled_ref[0:n, tcols] = part_r * ctf
            scaled_ref[n : 2 * n, tcols] = part_m * ctf
            inv = jnp.concatenate([inv_sigma[:, here]] * (ori_dev // 8), axis=0)
            for p, plane in enumerate((refs_r, refs_m)):
                weighted[p].append((plane * inv).astype(bf16))
                planes_ref[:, pl.ds(2 * col0 + p * chunk + t * lanes, lanes)] = plane.astype(bf16)
            power = jnp.concatenate([refs_r * refs_r + refs_m * refs_m, part_r * part_r + part_m * part_m], axis=0)
            high = power.astype(bf16).astype(f32)
            squares.append(jnp.concatenate([high, power - high], axis=0).astype(bf16))
        more = nt(jnp.concatenate(squares, axis=1), hot)
        norms = more if norms is None else norms + more
        for t in range(tiles):
            sine, cosine = sin_cos(phase_ref[:, pl.ds(col0 + t * lanes, lanes)])

            def store(p, i, value):
                at = 2 * col0 + p * chunk + t * lanes
                img_ref[i * trans : (i + 1) * trans, at : at + lanes] = value

            write_images(store, scaled_ref, col0 + t * lanes, cosine, sine, n)
        more = nt(img_ref[:, 2 * col0 : 2 * (col0 + chunk)], jnp.concatenate(weighted[0] + weighted[1], axis=1))
        scores = more if scores is None else scores + more

    both = ori_dev + part_dev
    norms = norms[0:both, :] + norms[both : 2 * both, :]
    ref_norm = norms[0:ori_dev]
    part_norm = norms[ori_dev:both]
    ctf_square = ctf_rows * ctf_rows
    energy = ref_norm / sigma
    quadratic = 0.5 * nt(ctf_square, energy, precision=highest)
    allowed = jnp.where(mask_ref[...] == 1, 1.0, 0.0)
    wide = (part_dev, trans, ori_dev)
    scores = scores.reshape(wide) - jnp.broadcast_to(quadratic[:, None, :], wide)
    scores = jnp.where(jnp.broadcast_to(allowed[:, None, :], wide) > 0.5, scores, -1e30)
    peak = jnp.max(jnp.max(scores, axis=1, keepdims=True), axis=2, keepdims=True)
    e = jnp.exp(scores - peak)
    orient_sums = jnp.sum(e, axis=1)
    e_wide = e.reshape(pairs, ori_dev)
    e_ref[...] = e_wide
    high = e_wide.astype(bf16)
    e_rows = jnp.concatenate([high.astype(f32), e_wide - high.astype(f32)], axis=1).astype(bf16)

    cross = None
    for step in range(blocks):
        col0 = step * chunk
        plane = planes_ref[:, 2 * col0 : 2 * (col0 + chunk)]
        mixed = nn(e_rows, jnp.concatenate([plane, plane], axis=0))
        total = None
        for p in range(2):
            at = 2 * col0 + p * chunk
            part = mixed[:, p * chunk : (p + 1) * chunk] * img_ref[:, at : at + chunk].astype(f32)
            total = part if total is None else total + part
        folded = total.reshape(part_dev, trans // 8, 8, chunk).sum(axis=1).reshape(part_dev * 8, chunk)
        more = nt(folded.astype(bf16), hot_ref[:, col0 : col0 + chunk])
        cross = more if cross is None else cross + more
    cross = cross.reshape(part_dev, 8, shells).sum(axis=1)
    total = jnp.sum(orient_sums, axis=1, keepdims=True)
    third = ctf_square * nn(orient_sums, ref_norm, precision=highest)
    noise = part_norm * total - 2.0 * cross + third
    lane = lax.broadcasted_iota(jnp.int32, (part_dev, lanes), 1)
    stat = jnp.concatenate([noise, jnp.zeros((part_dev, lanes - shells), f32)], axis=1)
    for k, piece in enumerate(pieces(peak.reshape(part_dev, 1), 3) + pieces(total, 3)):
        stat = jnp.where(lane == shells + k, jnp.broadcast_to(piece.astype(f32), lane.shape), stat)
    message = jnp.concatenate([e_wide.T, stat], axis=0).astype(bf16)

    def spread(dest, carry):
        message_ref[dest] = message
        return carry

    lax.fori_loop(0, message_ref.shape[0], spread, 0, unroll=8)


def column_kernel(
    group_ref,
    recv_hbm,
    phase_hbm,
    shell_hbm,
    table_hbm,
    img_hbm,
    square_hbm,
    recv_ref,
    phase_ref,
    shell_ref,
    table_ref,
    img_ref,
    square_ref,
    rows_ref,
    planes_ref,
    scaled_ref,
    ctf_ref,
    wave_ref,
    sems,
    out_sems,
):
    sources, part_dev, _, width = recv_ref.shape
    trans = phase_ref.shape[0]
    shells = table_ref.shape[1]
    pairs = part_dev * trans
    tiles = width // lanes
    start = pl.multiple_of(lax.axis_index("dom") * width, width)
    copies = start_all(
        [
            (table_hbm, table_ref),
            (shell_hbm.at[:, pl.ds(start, width)], shell_ref),
            (phase_hbm.at[:, pl.ds(start, width)], phase_ref),
            (recv_hbm, recv_ref),
        ],
        sems,
    )
    for copy in copies:
        copy.wait()
    for i in range(sources * part_dev):
        rows_ref[pl.ds(i, 1), :] = table_ref[pl.ds(group_ref[i], 1), :]
    hot = one_hot(shell_ref[...], shells)
    everyone = rows_ref[...]
    ctf_ref[...] = sum(nn(piece, hot) for piece in pieces(everyone, 3))
    square = everyone * everyone
    high = square.astype(bf16).astype(f32)
    squares = jnp.concatenate([high, square - high], axis=1)
    square_ref[...] = (
        jnp.broadcast_to(squares[:, None, :], (sources * part_dev, trans, 2 * shells))
        .reshape(sources * pairs, 2 * shells)
        .astype(bf16)
    )
    square_copy = pltpu.make_async_copy(square_ref, square_hbm, sems.at[0])
    square_copy.start()
    for t in range(tiles):
        cols = pl.ds(t * lanes, lanes)
        sine, cosine = sin_cos(phase_ref[:, cols])
        wave_ref[0:trans, cols] = cosine
        wave_ref[trans : 2 * trans, cols] = sine
    n = part_dev

    def source_step(src, carry):
        plane0 = pl.multiple_of(src * (tiles * part_dev * 2), tiles * part_dev * 2)
        split_planes((part_dev, tiles, lambda i, t: recv_ref[src, i, :, pl.ds(t * lanes, lanes)]), planes_ref, plane0)
        row0 = pl.multiple_of(src * pairs, pairs)
        mine = scaled_ref.at[pl.ds(pl.multiple_of(src * 2 * n, 2 * n), 2 * n), :]
        ctf_here = ctf_ref.at[pl.ds(pl.multiple_of(src * n, n), n), :]
        for t in range(tiles):
            cols = pl.ds(t * lanes, lanes)
            ctf = ctf_here[:, cols]
            mine[0:n, cols] = read_plane(planes_ref, plane0, part_dev, t, 0) * ctf
            mine[n : 2 * n, cols] = read_plane(planes_ref, plane0, part_dev, t, 1) * ctf
        for t in range(tiles):
            cols = pl.ds(t * lanes, lanes)

            def store(p, i, value):
                img_ref[p, pl.ds(row0 + i * trans, trans), cols] = value

            write_images(store, mine, t * lanes, wave_ref[0:trans, cols], wave_ref[trans : 2 * trans, cols], n)
        rows = pl.ds(row0, pairs)
        pltpu.make_async_copy(img_ref.at[:, rows, :], img_hbm.at[:, rows, :], out_sems.at[src]).start()
        return carry

    lax.fori_loop(0, sources, source_step, 0, unroll=2)

    def wait_step(src, carry):
        rows = pl.ds(pl.multiple_of(src * pairs, pairs), pairs)
        pltpu.make_async_copy(img_ref.at[:, rows, :], img_hbm.at[:, rows, :], out_sems.at[src]).wait()
        return carry

    lax.fori_loop(0, sources, wait_step, 0)
    square_copy.wait()


def sum_kernel(
    orients,
    shells,
    scale,
    img_hbm,
    square_hbm,
    recv_hbm,
    e_hbm,
    post_ref,
    sums_ref,
    weights_ref,
    noise_ref,
    img_ref,
    square_ref,
    recv_ref,
    e_ref,
    half_ref,
    share_ref,
    sems,
):
    pairs, ori_dev = e_ref.shape
    part_dev = recv_ref.shape[1] - ori_dev
    trans = pairs // part_dev
    sources = recv_ref.shape[0] // orients
    copies = start_all(
        [(recv_hbm, recv_ref), (e_hbm, e_ref), (square_hbm, square_ref), (img_hbm, img_ref)],
        sems,
    )
    me = lax.axis_index("dom")
    mine = lax.axis_index("orient")
    lane_part = lax.broadcasted_iota(jnp.int32, (part_dev, pairs), 1) // trans
    own = lane_part == lax.broadcasted_iota(jnp.int32, (part_dev, pairs), 0)
    row = lax.broadcasted_iota(jnp.int32, (lanes, 2 * lanes), 0) - shells
    upper = lax.broadcasted_iota(jnp.int32, (lanes, 2 * lanes), 1) // lanes
    picker = jnp.where((row >= 3 * upper) & (row < 3 * upper + 3), 1.0, 0.0).astype(bf16)

    copies[0].wait()
    stats = recv_ref[:, ori_dev : ori_dev + part_dev, :].astype(f32)
    rows = stats.reshape(sources * orients * part_dev, lanes).astype(bf16)
    decoded = nn(rows, picker)
    shape = (sources, orients, part_dev, lanes)
    peaks = decoded[:, 0:lanes].reshape(shape)
    totals = decoded[:, lanes : 2 * lanes].reshape(shape)
    shares = jnp.exp(peaks - jnp.max(peaks, axis=1, keepdims=True))
    shares = shares * (1.0 / jnp.sum(shares * totals, axis=1, keepdims=True))
    noise = jnp.sum(shares * stats.reshape(shape), axis=(0, 1))
    noise_ref[...] = jnp.sum(noise, axis=0, keepdims=True)[:, 0:shells] * scale
    share_ref[...] = shares.reshape(sources * orients, part_dev, lanes)
    for src in range(sources):
        factor = share_ref[src * orients + mine]
        lane = jnp.sum(jnp.where(own, factor, 0.0), axis=0, keepdims=True)
        post = recv_ref[src * orients + mine, 0:ori_dev, :].astype(f32) * lane
        high = post.astype(bf16).astype(f32)
        half_ref[:, pl.ds(src * pairs, pairs)] = jnp.concatenate([high, post - high], axis=0).astype(bf16)
    copies[1].wait()
    factor = share_ref[me * orients + mine][:, 0:ori_dev]
    wide = (part_dev, trans, ori_dev)
    post_ref[...] = (e_ref[...].reshape(wide) * jnp.broadcast_to(factor[:, None, :], wide)).reshape(pairs, ori_dev)
    half = half_ref[...]
    copies[2].wait()
    weights = nn(half, square_ref[...])
    weights = weights[0:ori_dev] + weights[ori_dev : 2 * ori_dev]
    weights_ref[...] = weights[:, 0:shells] + weights[:, shells : 2 * shells]
    copies[3].wait()
    for p in range(2):
        sums = nn(half, img_ref[p])
        sums = sums[0:ori_dev] + sums[ori_dev : 2 * ori_dev]
        for j in range(ori_dev):
            sums_ref[j, p : p + 1, :] = sums[j : j + 1, :]


def on_device(particles, references, phases, mask, ctf_group, ctf_table, shell_index, sigma2):
    part_dev, _, pixels = particles.shape
    ori_dev = references.shape[0]
    trans = phases.shape[0]
    shells = ctf_table.shape[1]
    dom = lax.axis_size("dom")
    orients = lax.axis_size("orient")
    width = pixels // dom
    pairs = part_dev * trans
    chunk = 512
    groups = 4
    shell_row = shell_index.reshape(1, pixels)
    sigma_row = sigma2.reshape(1, shells)
    vmem = pl.BlockSpec(memory_space=pltpu.VMEM)
    smem = pl.BlockSpec(memory_space=pltpu.SMEM)
    anywhere = pl.BlockSpec(memory_space=pl.ANY)
    params = pltpu.CompilerParams(vmem_limit_bytes=vmem_bytes)
    dma = pltpu.SemaphoreType.DMA

    send = pl.pallas_call(
        pack_kernel,
        out_shape=jax.ShapeDtypeStruct((dom, part_dev, 2, width), bf16),
        in_specs=[anywhere],
        out_specs=anywhere,
        scratch_shapes=[pltpu.VMEM((dom, part_dev, 2, width), bf16), dma((dom,)), dma((dom,))],
        compiler_params=params,
        name="pack",
    )(particles)
    recv = lax.all_to_all(send, "dom", 0, 0)

    both = ori_dev + part_dev
    message, e = pl.pallas_call(
        functools.partial(score_kernel, chunk, groups),
        out_shape=(
            jax.ShapeDtypeStruct((dom * orients, both, lanes), bf16),
            jax.ShapeDtypeStruct((pairs, ori_dev), f32),
        ),
        in_specs=[smem] + [anywhere] * 7,
        out_specs=(vmem, vmem),
        scratch_shapes=[
            pltpu.VMEM(particles.shape, bf16),
            pltpu.VMEM(references.shape, bf16),
            pltpu.VMEM(phases.shape, f32),
            pltpu.VMEM((1, pixels), jnp.int32),
            pltpu.VMEM(mask.shape, jnp.int32),
            pltpu.VMEM(ctf_table.shape, f32),
            pltpu.VMEM((1, shells), f32),
            pltpu.VMEM((pixels // lanes * part_dev * 2, lanes), f32),
            pltpu.VMEM((pixels // lanes * ori_dev * 2, lanes), f32),
            pltpu.VMEM((pairs, 2 * pixels), bf16),
            pltpu.VMEM((ori_dev, 2 * pixels), bf16),
            pltpu.VMEM((shells, pixels), bf16),
            pltpu.VMEM((2 * part_dev, pixels), f32),
            pltpu.VMEM((part_dev, shells), f32),
            dma((4,)),
            dma((groups, 3)),
        ],
        compiler_params=params,
        name="scores",
    )(ctf_group, particles, references, phases, shell_row, mask, ctf_table, sigma_row)

    messages = lax.all_to_all(message, ("dom", "orient"), 0, 0)

    images, squares = pl.pallas_call(
        column_kernel,
        out_shape=(
            jax.ShapeDtypeStruct((2, dom * pairs, width), bf16),
            jax.ShapeDtypeStruct((dom * pairs, 2 * shells), bf16),
        ),
        in_specs=[smem] + [anywhere] * 4,
        out_specs=(anywhere, anywhere),
        scratch_shapes=[
            pltpu.VMEM((dom, part_dev, 2, width), bf16),
            pltpu.VMEM((trans, width), f32),
            pltpu.VMEM((1, width), jnp.int32),
            pltpu.VMEM(ctf_table.shape, f32),
            pltpu.VMEM((2, dom * pairs, width), bf16),
            pltpu.VMEM((dom * pairs, 2 * shells), bf16),
            pltpu.VMEM((dom * part_dev, shells), f32),
            pltpu.VMEM((dom * part_dev * 2 * width // lanes, lanes), f32),
            pltpu.VMEM((dom * part_dev * 2, width), f32),
            pltpu.VMEM((dom * part_dev, width), f32),
            pltpu.VMEM((2 * trans, width), f32),
            dma((4,)),
            dma((dom,)),
        ],
        compiler_params=params,
        name="columns",
    )(ctf_group, recv, phases, shell_row, ctf_table)

    scale = shells / (part_dev * dom * pixels)
    posterior, image_sums, ctf_weights, noise = pl.pallas_call(
        functools.partial(sum_kernel, orients, shells, scale),
        out_shape=(
            jax.ShapeDtypeStruct((pairs, ori_dev), f32),
            jax.ShapeDtypeStruct((ori_dev, 2, width), f32),
            jax.ShapeDtypeStruct((ori_dev, shells), f32),
            jax.ShapeDtypeStruct((1, shells), f32),
        ),
        in_specs=[anywhere] * 4,
        out_specs=(vmem, vmem, vmem, vmem),
        scratch_shapes=[
            pltpu.VMEM((2, dom * pairs, width), bf16),
            pltpu.VMEM((dom * pairs, 2 * shells), bf16),
            pltpu.VMEM((dom * orients, both, lanes), bf16),
            pltpu.VMEM((pairs, ori_dev), f32),
            pltpu.VMEM((2 * ori_dev, dom * pairs), bf16),
            pltpu.VMEM((dom * orients, part_dev, lanes), f32),
            dma((4,)),
        ],
        compiler_params=params,
        name="sums",
    )(images, squares, messages, e)
    return (
        posterior.reshape(part_dev, trans, ori_dev),
        image_sums,
        ctf_weights,
        noise.reshape(shells),
    )


def solution(mesh):
    return jax.shard_map(
        on_device,
        mesh=mesh,
        in_specs=(
            P("dom", None, None),
            P("orient", None, None),
            P(),
            P("dom", "orient"),
            P(),
            P(),
            P(),
            P(),
        ),
        out_specs=(P("dom", None, "orient"), P("orient", None, "dom"), P("orient", None), P()),
        check_vma=False,
    )
```

```python
import functools

import jax
import jax.numpy as jnp
from jax import lax
from jax.experimental import pallas as pl
from jax.experimental.pallas import tpu as pltpu
from jax.sharding import PartitionSpec as P

f32 = jnp.float32
bf16 = jnp.bfloat16
highest = lax.Precision.HIGHEST
lanes = 128
wave_tile = 256

sin_terms = (0.9999999766, -0.1666664762, 0.008332899654, -0.000198008873, 2.590467297e-06)
cos_terms = (0.9999999998, -0.4999999936, 0.04166663624, -0.001388836119, 2.47601506e-05, -2.605130157e-07)


def horner(terms, z):
    total = terms[-1] * z + terms[-2]
    for term in terms[-3::-1]:
        total = total * z + term
    return total


def sin_cos(angle):
    half = angle * 0.5
    z = half * half
    s = half * horner(sin_terms, z)
    c = horner(cos_terms, z)
    twice = s + s
    return twice * c, 1.0 - twice * s


def pieces(x, count):
    out = []
    rest = x
    for step in range(count):
        piece = rest.astype(bf16)
        out.append(piece)
        if step + 1 < count:
            rest = rest - piece.astype(f32)
    return out


def nt(a, b, **kw):
    return lax.dot_general(a, b, (((1,), (1,)), ((), ())), preferred_element_type=f32, **kw)


def tn(a, b, **kw):
    return lax.dot_general(a, b, (((0,), (0,)), ((), ())), preferred_element_type=f32, **kw)


def nn(a, b, **kw):
    return lax.dot_general(a, b, (((1,), (0,)), ((), ())), preferred_element_type=f32, **kw)


def one_hot(index_row, shells):
    rows = lax.broadcasted_iota(jnp.int32, (shells, index_row.shape[1]), 0)
    return jnp.where(rows == index_row, 1.0, 0.0).astype(bf16)


def start_all(pairs, sems):
    copies = [pltpu.make_async_copy(src, dst, sems.at[k]) for k, (src, dst) in enumerate(pairs)]
    for copy in copies:
        copy.start()
    return copies


def split_planes(src, dst_ref, row0):
    items, tiles, load = src
    for tile in range(tiles):
        for item in range(items):
            dst_ref[pl.ds(row0 + (tile * items + item) * 2, 2), :] = load(item, tile).astype(f32)


def read_plane(ref, row0, items, tile, plane):
    return ref[pl.ds(row0 + tile * items * 2 + plane, items, 2), :]


def write_images(store, scaled_ref, scaled_col, cosine, sine, count):
    trans = cosine.shape[0]
    cols = pl.ds(scaled_col, lanes)
    for i in range(count):
        r = jnp.broadcast_to(scaled_ref[i : i + 1, cols], (trans, lanes))
        m = jnp.broadcast_to(scaled_ref[count + i : count + i + 1, cols], (trans, lanes))
        store(0, i, (r * cosine - m * sine).astype(bf16))
        store(1, i, (r * sine + m * cosine).astype(bf16))


def pack_kernel(part_hbm, out_ref, sems):
    dests, _, _, width = out_ref.shape
    copies = start_all(
        [(part_hbm.at[:, :, pl.ds(dest * width, width)], out_ref.at[dest]) for dest in range(dests)], sems
    )
    for copy in copies:
        copy.wait()


def score_kernel(
    chunk,
    groups,
    group_hbm,
    part_hbm,
    refs_hbm,
    phase_hbm,
    shell_hbm,
    mask_hbm,
    table_hbm,
    sigma_hbm,
    message_ref,
    e_ref,
    part_ref,
    refs_ref,
    phase_ref,
    shell_ref,
    mask_ref,
    table_ref,
    sigma_ref,
    group_ref,
    part_rows,
    refs_rows,
    img_ref,
    planes_ref,
    hot_ref,
    scaled_ref,
    rows_ref,
    small_sems,
    big_sems,
):
    part_dev, _, pixels = part_ref.shape
    ori_dev = refs_ref.shape[0]
    trans = phase_ref.shape[0]
    shells = table_ref.shape[1]
    pairs = part_dev * trans
    blocks = pixels // chunk
    tiles = chunk // lanes
    first = lax.axis_index("dom") * part_dev
    small = start_all(
        [
            (group_hbm, group_ref),
            (table_hbm, table_ref),
            (sigma_hbm, sigma_ref),
            (shell_hbm, shell_ref),
            (mask_hbm, mask_ref),
        ],
        small_sems,
    )
    big = []
    for g in range(groups):
        cols = pl.ds(g * (pixels // groups), pixels // groups)
        big.append(
            start_all(
                [
                    (part_hbm.at[:, :, cols], part_ref.at[:, :, cols]),
                    (phase_hbm.at[:, cols], phase_ref.at[:, cols]),
                    (refs_hbm.at[:, :, cols], refs_ref.at[:, :, cols]),
                ],
                big_sems.at[g],
            )
        )
    for copy in small:
        copy.wait()

    for i in range(part_dev):
        rows_ref[pl.ds(i, 1), :] = table_ref[pl.ds(group_ref[first + i], 1), :]
    ctf_rows = rows_ref[...]
    sigma = sigma_ref[...]
    inverse = jnp.broadcast_to(1.0 / sigma, (8, shells))
    table = jnp.concatenate(
        [p.astype(f32) for p in pieces(ctf_rows, 3)] + [p.astype(f32) for p in pieces(inverse, 3)], axis=0
    ).astype(bf16)
    n = part_dev
    norms = None
    scores = None
    for step in range(blocks):
        if step % (blocks // groups) == 0:
            for copy in big[step // (blocks // groups)]:
                copy.wait()
        col0 = step * chunk
        cols = pl.ds(col0, chunk)
        hot = one_hot(shell_ref[:, cols], shells)
        hot_ref[:, cols] = hot
        picked = nn(table, hot)
        ctf_pix = picked[0:n] + picked[n : 2 * n] + picked[2 * n : 3 * n]
        inv_sigma = picked[3 * n : 3 * n + 8] + picked[3 * n + 8 : 3 * n + 16] + picked[3 * n + 16 : 3 * n + 24]
        part0 = step * tiles * part_dev * 2
        refs0 = step * tiles * ori_dev * 2
        split_planes((part_dev, tiles, lambda i, t: part_ref[i, :, pl.ds(col0 + t * lanes, lanes)]), part_rows, part0)
        split_planes((ori_dev, tiles, lambda j, t: refs_ref[j, :, pl.ds(col0 + t * lanes, lanes)]), refs_rows, refs0)
        squares = []
        weighted = [[], []]
        for t in range(tiles):
            here = slice(t * lanes, (t + 1) * lanes)
            tcols = pl.ds(col0 + t * lanes, lanes)
            part_r = read_plane(part_rows, part0, part_dev, t, 0)
            part_m = read_plane(part_rows, part0, part_dev, t, 1)
            refs_r = read_plane(refs_rows, refs0, ori_dev, t, 0)
            refs_m = read_plane(refs_rows, refs0, ori_dev, t, 1)
            ctf = ctf_pix[:, here]
            scaled_ref[0:n, tcols] = part_r * ctf
            scaled_ref[n : 2 * n, tcols] = part_m * ctf
            inv = jnp.concatenate([inv_sigma[:, here]] * (ori_dev // 8), axis=0)
            for p, plane in enumerate((refs_r, refs_m)):
                weighted[p].append((plane * inv).astype(bf16))
                planes_ref[:, pl.ds(2 * col0 + p * chunk + t * lanes, lanes)] = plane.astype(bf16)
            power = jnp.concatenate([refs_r * refs_r + refs_m * refs_m, part_r * part_r + part_m * part_m], axis=0)
            high = power.astype(bf16).astype(f32)
            squares.append(jnp.concatenate([high, power - high], axis=0).astype(bf16))
        more = nt(jnp.concatenate(squares, axis=1), hot)
        norms = more if norms is None else norms + more
        for t in range(tiles):
            sine, cosine = sin_cos(phase_ref[:, pl.ds(col0 + t * lanes, lanes)])

            def store(p, i, value):
                at = 2 * col0 + p * chunk + t * lanes
                img_ref[i * trans : (i + 1) * trans, at : at + lanes] = value

            write_images(store, scaled_ref, col0 + t * lanes, cosine, sine, n)
        more = nt(img_ref[:, 2 * col0 : 2 * (col0 + chunk)], jnp.concatenate(weighted[0] + weighted[1], axis=1))
        scores = more if scores is None else scores + more

    both = ori_dev + part_dev
    norms = norms[0:both, :] + norms[both : 2 * both, :]
    ref_norm = norms[0:ori_dev]
    part_norm = norms[ori_dev:both]
    ctf_square = ctf_rows * ctf_rows
    energy = ref_norm / sigma
    quadratic = 0.5 * nt(ctf_square, energy, precision=highest)
    allowed = jnp.where(mask_ref[...] == 1, 1.0, 0.0)
    wide = (part_dev, trans, ori_dev)
    scores = scores.reshape(wide) - jnp.broadcast_to(quadratic[:, None, :], wide)
    scores = jnp.where(jnp.broadcast_to(allowed[:, None, :], wide) > 0.5, scores, -1e30)
    peak = jnp.max(jnp.max(scores, axis=1, keepdims=True), axis=2, keepdims=True)
    e = jnp.exp(scores - peak)
    orient_sums = jnp.sum(e, axis=1)
    e_wide = e.reshape(pairs, ori_dev)
    e_ref[...] = e_wide
    high = e_wide.astype(bf16)
    e_rows = jnp.concatenate([high.astype(f32), e_wide - high.astype(f32)], axis=1).astype(bf16)

    cross = None
    for step in range(blocks):
        col0 = step * chunk
        plane = planes_ref[:, 2 * col0 : 2 * (col0 + chunk)]
        mixed = nn(e_rows, jnp.concatenate([plane, plane], axis=0))
        total = None
        for p in range(2):
            at = 2 * col0 + p * chunk
            part = mixed[:, p * chunk : (p + 1) * chunk] * img_ref[:, at : at + chunk].astype(f32)
            total = part if total is None else total + part
        folded = total.reshape(part_dev, trans // 8, 8, chunk).sum(axis=1).reshape(part_dev * 8, chunk)
        more = nt(folded.astype(bf16), hot_ref[:, col0 : col0 + chunk])
        cross = more if cross is None else cross + more
    cross = cross.reshape(part_dev, 8, shells).sum(axis=1)
    total = jnp.sum(orient_sums, axis=1, keepdims=True)
    third = ctf_square * nn(orient_sums, ref_norm, precision=highest)
    noise = part_norm * total - 2.0 * cross + third
    lane = lax.broadcasted_iota(jnp.int32, (part_dev, lanes), 1)
    stat = jnp.concatenate([noise, jnp.zeros((part_dev, lanes - shells), f32)], axis=1)
    for k, piece in enumerate(pieces(peak.reshape(part_dev, 1), 3) + pieces(total, 3)):
        stat = jnp.where(lane == shells + k, jnp.broadcast_to(piece.astype(f32), lane.shape), stat)
    message = jnp.concatenate([e_wide.T, stat], axis=0).astype(bf16)

    def spread(dest, carry):
        message_ref[dest] = message
        return carry

    lax.fori_loop(0, message_ref.shape[0], spread, 0, unroll=8)


def column_kernel(
    group_hbm,
    recv_ref,
    phase_hbm,
    shell_hbm,
    table_hbm,
    scaled_hbm,
    wave_hbm,
    square_hbm,
    group_ref,
    phase_ref,
    shell_ref,
    table_ref,
    scaled_ref,
    wave_ref,
    square_ref,
    rows_ref,
    planes_ref,
    ctf_ref,
    sems,
):
    sources, part_dev, _, width = recv_ref.shape
    trans = phase_ref.shape[0]
    shells = table_ref.shape[1]
    pairs = part_dev * trans
    tiles = width // lanes
    span = wave_tile // lanes
    start = pl.multiple_of(lax.axis_index("dom") * width, width)
    copies = start_all(
        [
            (group_hbm, group_ref),
            (table_hbm, table_ref),
            (shell_hbm.at[:, pl.ds(start, width)], shell_ref),
            (phase_hbm.at[:, pl.ds(start, width)], phase_ref),
        ],
        sems,
    )
    for copy in copies:
        copy.wait()
    for i in range(sources * part_dev):
        rows_ref[pl.ds(i, 1), :] = table_ref[pl.ds(group_ref[i], 1), :]
    hot = one_hot(shell_ref[...], shells)
    everyone = rows_ref[...]
    ctf_ref[...] = sum(nn(piece, hot) for piece in pieces(everyone, 3))
    for t in range(tiles):
        at = (t // span * 2 * span + t % span) * lanes
        sine, cosine = sin_cos(phase_ref[:, pl.ds(t * lanes, lanes)])
        for wave, offset in ((cosine, at), (sine, at + wave_tile)):
            high = wave.astype(bf16)
            wave_ref[0:trans, pl.ds(offset, lanes)] = high
            wave_ref[trans : 2 * trans, pl.ds(offset, lanes)] = (wave - high.astype(f32)).astype(bf16)
    square = everyone * everyone
    high = square.astype(bf16).astype(f32)
    squares = jnp.concatenate([high, square - high], axis=1)
    square_ref[...] = (
        jnp.broadcast_to(squares[:, None, :], (sources * part_dev, trans, 2 * shells))
        .reshape(sources * pairs, 2 * shells)
        .astype(bf16)
    )
    n = part_dev

    def source_step(src, carry):
        plane0 = pl.multiple_of(src * (tiles * part_dev * 2), tiles * part_dev * 2)
        split_planes((part_dev, tiles, lambda i, t: recv_ref[src, i, :, pl.ds(t * lanes, lanes)]), planes_ref, plane0)
        rows = pl.ds(pl.multiple_of(src * n, n), n)
        for t in range(tiles):
            cols = pl.ds(t * lanes, lanes)
            ctf = ctf_ref[rows, cols]
            for p in range(2):
                scaled_ref[p, rows, cols] = read_plane(planes_ref, plane0, part_dev, t, p) * ctf
        return carry

    lax.fori_loop(0, sources, source_step, 0, unroll=2)
    copies = start_all([(scaled_ref, scaled_hbm), (wave_ref, wave_hbm), (square_ref, square_hbm)], sems)
    for copy in copies:
        copy.wait()


def sum_kernel(
    orients,
    shells,
    scale,
    scaled_hbm,
    wave_hbm,
    square_hbm,
    recv_ref,
    e_ref,
    post_ref,
    sums_ref,
    weights_ref,
    noise_ref,
    scaled_ref,
    wave_ref,
    square_ref,
    half_ref,
    left_ref,
    share_ref,
    sems,
):
    pairs, ori_dev = e_ref.shape
    part_dev = recv_ref.shape[1] - ori_dev
    trans = pairs // part_dev
    sources = recv_ref.shape[0] // orients
    copies = start_all([(wave_hbm, wave_ref), (scaled_hbm, scaled_ref), (square_hbm, square_ref)], sems)
    me = lax.axis_index("dom")
    mine = lax.axis_index("orient")
    lane_part = lax.broadcasted_iota(jnp.int32, (part_dev, pairs), 1) // trans
    own = lane_part == lax.broadcasted_iota(jnp.int32, (part_dev, pairs), 0)
    lane = lax.broadcasted_iota(jnp.int32, (ori_dev, pairs), 1)
    lower = lane < pairs // 2
    half_part = lane % (pairs // 2) // trans
    row = lax.broadcasted_iota(jnp.int32, (lanes, 2 * lanes), 0) - shells
    upper = lax.broadcasted_iota(jnp.int32, (lanes, 2 * lanes), 1) // lanes
    picker = jnp.where((row >= 3 * upper) & (row < 3 * upper + 3), 1.0, 0.0).astype(bf16)

    stats = recv_ref[:, ori_dev : ori_dev + part_dev, :].astype(f32)
    rows = stats.reshape(sources * orients * part_dev, lanes).astype(bf16)
    decoded = nn(rows, picker)
    shape = (sources, orients, part_dev, lanes)
    peaks = decoded[:, 0:lanes].reshape(shape)
    totals = decoded[:, lanes : 2 * lanes].reshape(shape)
    shares = jnp.exp(peaks - jnp.max(peaks, axis=1, keepdims=True))
    shares = shares * (1.0 / jnp.sum(shares * totals, axis=1, keepdims=True))
    noise = jnp.sum(shares * stats.reshape(shape), axis=(0, 1))
    noise_ref[...] = jnp.sum(noise, axis=0, keepdims=True)[:, 0:shells] * scale
    share_ref[...] = shares.reshape(sources * orients, part_dev, lanes)
    for src in range(sources):
        factor = share_ref[src * orients + mine]
        lane = jnp.sum(jnp.where(own, factor, 0.0), axis=0, keepdims=True)
        post = recv_ref[src * orients + mine, 0:ori_dev, :].astype(f32) * lane
        high = post.astype(bf16).astype(f32)
        low = post - high
        half_ref[:, pl.ds(src * pairs, pairs)] = jnp.concatenate([high, low], axis=0).astype(bf16)
        turned = [pltpu.roll(x, pairs // 2, 1) for x in (high, low)]
        mixes = (jnp.where(lower, high, turned[1]), jnp.where(lower, turned[0], low))
        highs = (high, turned[0])
        for i in range(part_dev):
            rows = pl.ds((src * part_dev + i) * ori_dev, ori_dev)
            group = i // (part_dev // 2)
            here = half_part == i % (part_dev // 2)
            left_ref[rows, 0:pairs] = jnp.where(here, mixes[group], 0.0).astype(bf16)
            left_ref[rows, pairs : 2 * pairs] = jnp.where(here & lower, highs[group], 0.0).astype(bf16)
    factor = share_ref[me * orients + mine][:, 0:ori_dev]
    wide = (part_dev, trans, ori_dev)
    post_ref[...] = (e_ref[...].reshape(wide) * jnp.broadcast_to(factor[:, None, :], wide)).reshape(pairs, ori_dev)
    copies[0].wait()
    copies[1].wait()
    for tile in range(sums_ref.shape[2] // wave_tile):
        cols = slice(tile * wave_tile, (tile + 1) * wave_tile)
        waves = wave_ref[:, 2 * tile * wave_tile : 2 * (tile + 1) * wave_tile]
        high = waves[0:trans]
        low = waves[trans : 2 * trans]
        mixed = nn(left_ref[...], jnp.concatenate([high] * part_dev + [low] * part_dev, axis=0))
        sums = [None, None]
        for i in range(sources * part_dev):
            block = mixed[i * ori_dev : (i + 1) * ori_dev]
            cosine = block[:, 0:wave_tile]
            sine = block[:, wave_tile : 2 * wave_tile]
            r = jnp.broadcast_to(scaled_ref[0, i : i + 1, cols], cosine.shape)
            m = jnp.broadcast_to(scaled_ref[1, i : i + 1, cols], cosine.shape)
            more = (r * cosine - m * sine, r * sine + m * cosine)
            sums = [new if old is None else old + new for old, new in zip(sums, more)]
        for p in range(2):
            for j in range(ori_dev):
                sums_ref[j, p : p + 1, cols] = sums[p][j : j + 1, :]
    copies[2].wait()
    weights = nn(half_ref[...], square_ref[...])
    weights = weights[0:ori_dev] + weights[ori_dev : 2 * ori_dev]
    weights_ref[...] = weights[:, 0:shells] + weights[:, shells : 2 * shells]


def on_device(particles, references, phases, mask, ctf_group, ctf_table, shell_index, sigma2):
    part_dev, _, pixels = particles.shape
    ori_dev = references.shape[0]
    trans = phases.shape[0]
    shells = ctf_table.shape[1]
    dom = lax.axis_size("dom")
    orients = lax.axis_size("orient")
    width = pixels // dom
    pairs = part_dev * trans
    chunk = 2048
    groups = 1
    shell_row = shell_index.reshape(1, pixels)
    sigma_row = sigma2.reshape(1, shells)
    vmem = pl.BlockSpec(memory_space=pltpu.VMEM)
    smem = pl.BlockSpec(memory_space=pltpu.SMEM)
    anywhere = pl.BlockSpec(memory_space=pl.ANY)
    params = pltpu.CompilerParams(vmem_limit_bytes=20 * 1024 * 1024)
    far = lambda x: pltpu.with_memory_space_constraint(x, pltpu.HBM)
    dma = pltpu.SemaphoreType.DMA

    send = pl.pallas_call(
        pack_kernel,
        out_shape=pltpu.VMEM((dom, part_dev, 2, width), bf16),
        in_specs=[anywhere],
        out_specs=vmem,
        scratch_shapes=[dma((dom,))],
        compiler_params=params,
        name="pack",
    )(far(particles))
    recv = lax.all_to_all(send, "dom", 0, 0)

    both = ori_dev + part_dev
    message, e = pl.pallas_call(
        functools.partial(score_kernel, chunk, groups),
        out_shape=(
            jax.ShapeDtypeStruct((dom * orients, both, lanes), bf16),
            jax.ShapeDtypeStruct((pairs, ori_dev), f32),
        ),
        in_specs=[anywhere] * 8,
        out_specs=(vmem, vmem),
        scratch_shapes=[
            pltpu.VMEM(particles.shape, bf16),
            pltpu.VMEM(references.shape, bf16),
            pltpu.VMEM(phases.shape, f32),
            pltpu.VMEM((1, pixels), jnp.int32),
            pltpu.VMEM(mask.shape, jnp.int32),
            pltpu.VMEM(ctf_table.shape, f32),
            pltpu.VMEM((1, shells), f32),
            pltpu.SMEM(ctf_group.shape, jnp.int32),
            pltpu.VMEM((pixels // lanes * part_dev * 2, lanes), f32),
            pltpu.VMEM((pixels // lanes * ori_dev * 2, lanes), f32),
            pltpu.VMEM((pairs, 2 * pixels), bf16),
            pltpu.VMEM((ori_dev, 2 * pixels), bf16),
            pltpu.VMEM((shells, pixels), bf16),
            pltpu.VMEM((2 * part_dev, pixels), f32),
            pltpu.VMEM((part_dev, shells), f32),
            dma((5,)),
            dma((groups, 3)),
        ],
        compiler_params=params,
        name="scores",
    )(
        far(ctf_group),
        far(particles),
        far(references),
        far(phases),
        far(shell_row),
        far(mask),
        far(ctf_table),
        far(sigma_row),
    )

    messages = lax.all_to_all(message, ("dom", "orient"), 0, 0)

    particles_all = dom * part_dev
    columns = (
        ((2, particles_all, width), f32),
        ((2 * trans, 2 * width), bf16),
        ((particles_all * trans, 2 * shells), bf16),
    )
    scaled, waves, squares = pl.pallas_call(
        column_kernel,
        out_shape=tuple(pltpu.HBM(*column) for column in columns),
        in_specs=[anywhere, vmem] + [anywhere] * 3,
        out_specs=(anywhere,) * 3,
        scratch_shapes=[
            pltpu.SMEM(ctf_group.shape, jnp.int32),
            pltpu.VMEM((trans, width), f32),
            pltpu.VMEM((1, width), jnp.int32),
            pltpu.VMEM(ctf_table.shape, f32),
        ]
        + [pltpu.VMEM(*column) for column in columns]
        + [
            pltpu.VMEM((particles_all, shells), f32),
            pltpu.VMEM((particles_all * 2 * width // lanes, lanes), f32),
            pltpu.VMEM((particles_all, width), f32),
            dma((4,)),
        ],
        compiler_params=params,
        name="columns",
    )(far(ctf_group), recv, far(phases), far(shell_row), far(ctf_table))

    scale = shells / (part_dev * dom * pixels)
    posterior, image_sums, ctf_weights, noise = pl.pallas_call(
        functools.partial(sum_kernel, orients, shells, scale),
        out_shape=(
            jax.ShapeDtypeStruct((pairs, ori_dev), f32),
            jax.ShapeDtypeStruct((ori_dev, 2, width), f32),
            jax.ShapeDtypeStruct((ori_dev, shells), f32),
            jax.ShapeDtypeStruct((1, shells), f32),
        ),
        in_specs=[anywhere, anywhere, anywhere, vmem, vmem],
        out_specs=(vmem, vmem, vmem, vmem),
        scratch_shapes=[pltpu.VMEM(*column) for column in columns]
        + [
            pltpu.VMEM((2 * ori_dev, particles_all * trans), bf16),
            pltpu.VMEM((particles_all * ori_dev, 2 * pairs), bf16),
            pltpu.VMEM((dom * orients, part_dev, lanes), f32),
            dma((3,)),
        ],
        compiler_params=params,
        name="sums",
    )(far(scaled), far(waves), far(squares), messages, e)
    return (
        posterior.reshape(part_dev, trans, ori_dev),
        image_sums,
        ctf_weights,
        noise.reshape(shells),
    )


def solution(mesh):
    return jax.shard_map(
        on_device,
        mesh=mesh,
        in_specs=(
            P("dom", None, None),
            P("orient", None, None),
            P(),
            P("dom", "orient"),
            P(),
            P(),
            P(),
            P(),
        ),
        out_specs=(P("dom", None, "orient"), P("orient", None, "dom"), P("orient", None), P()),
        check_vma=False,
    )
```

```python
import functools

import jax
import jax.numpy as jnp
from jax import lax
from jax.experimental import pallas as pl
from jax.experimental.pallas import tpu as pltpu
from jax.sharding import PartitionSpec as P

f32 = jnp.float32
bf16 = jnp.bfloat16
highest = lax.Precision.HIGHEST
lanes = 128
wave_tile = 256

sin_terms = (0.9999999766, -0.1666664762, 0.008332899654, -0.000198008873, 2.590467297e-06)
cos_terms = (0.9999999998, -0.4999999936, 0.04166663624, -0.001388836119, 2.47601506e-05, -2.605130157e-07)


def horner(terms, z):
    total = terms[-1] * z + terms[-2]
    for term in terms[-3::-1]:
        total = total * z + term
    return total


def sin_cos(angle):
    half = angle * 0.5
    z = half * half
    s = half * horner(sin_terms, z)
    c = horner(cos_terms, z)
    twice = s + s
    return twice * c, 1.0 - twice * s


def pieces(x, count):
    out = []
    rest = x
    for step in range(count):
        piece = rest.astype(bf16)
        out.append(piece)
        if step + 1 < count:
            rest = rest - piece.astype(f32)
    return out


def nt(a, b, **kw):
    return lax.dot_general(a, b, (((1,), (1,)), ((), ())), preferred_element_type=f32, **kw)


def tn(a, b, **kw):
    return lax.dot_general(a, b, (((0,), (0,)), ((), ())), preferred_element_type=f32, **kw)


def nn(a, b, **kw):
    return lax.dot_general(a, b, (((1,), (0,)), ((), ())), preferred_element_type=f32, **kw)


def one_hot(index_row, shells):
    rows = lax.broadcasted_iota(jnp.int32, (shells, index_row.shape[1]), 0)
    return jnp.where(rows == index_row, 1.0, 0.0).astype(bf16)


def start_all(pairs, sems):
    copies = [pltpu.make_async_copy(src, dst, sems.at[k]) for k, (src, dst) in enumerate(pairs)]
    for copy in copies:
        copy.start()
    return copies


def split_planes(src, dst_ref, row0):
    items, tiles, load = src
    for tile in range(tiles):
        for item in range(items):
            dst_ref[pl.ds(row0 + (tile * items + item) * 2, 2), :] = load(item, tile).astype(f32)


def read_plane(ref, row0, items, tile, plane):
    return ref[pl.ds(row0 + tile * items * 2 + plane, items, 2), :]


def write_images(store, scaled_ref, scaled_col, cosine, sine, count):
    trans = cosine.shape[0]
    cols = pl.ds(scaled_col, lanes)
    for i in range(count):
        r = jnp.broadcast_to(scaled_ref[i : i + 1, cols], (trans, lanes))
        m = jnp.broadcast_to(scaled_ref[count + i : count + i + 1, cols], (trans, lanes))
        store(0, i, (r * cosine - m * sine).astype(bf16))
        store(1, i, (r * sine + m * cosine).astype(bf16))


def pack_kernel(part_hbm, out_ref, sems):
    dests, _, _, width = out_ref.shape
    copies = start_all(
        [(part_hbm.at[:, :, pl.ds(dest * width, width)], out_ref.at[dest]) for dest in range(dests)], sems
    )
    for copy in copies:
        copy.wait()


def score_kernel(
    chunk,
    group_hbm,
    part_hbm,
    refs_hbm,
    phase_hbm,
    shell_hbm,
    mask_hbm,
    table_hbm,
    sigma_hbm,
    message_ref,
    e_ref,
    part_ref,
    refs_ref,
    phase_ref,
    shell_ref,
    mask_ref,
    table_ref,
    sigma_ref,
    group_ref,
    part_rows,
    refs_rows,
    img_ref,
    planes_ref,
    hot_ref,
    scaled_ref,
    pix_ref,
    wave_ref,
    rows_ref,
    small_sems,
    big_sems,
):
    part_dev, _, pixels = part_ref.shape
    ori_dev = refs_ref.shape[0]
    trans = phase_ref.shape[0]
    shells = table_ref.shape[1]
    pairs = part_dev * trans
    blocks = pixels // chunk
    tiles = chunk // lanes
    first = lax.axis_index("dom") * part_dev
    small = start_all(
        [
            (group_hbm, group_ref),
            (table_hbm, table_ref),
            (sigma_hbm, sigma_ref),
            (shell_hbm, shell_ref),
            (mask_hbm, mask_ref),
        ],
        small_sems,
    )
    big = start_all([(phase_hbm, phase_ref), (part_hbm, part_ref), (refs_hbm, refs_ref)], big_sems)
    for copy in small:
        copy.wait()

    for i in range(part_dev):
        rows_ref[pl.ds(i, 1), :] = table_ref[pl.ds(group_ref[first + i], 1), :]
    ctf_rows = rows_ref[...]
    sigma = sigma_ref[...]
    inverse = jnp.broadcast_to(1.0 / sigma, (8, shells))
    table = jnp.concatenate(
        [p.astype(f32) for p in pieces(ctf_rows, 3)] + [p.astype(f32) for p in pieces(inverse, 3)], axis=0
    ).astype(bf16)
    n = part_dev
    for step in range(blocks):
        cols = slice(step * chunk, (step + 1) * chunk)
        hot = one_hot(shell_ref[:, cols], shells)
        hot_ref[:, cols] = hot
        picked = nn(table, hot)
        pix_ref[0:n, cols] = picked[0:n] + picked[n : 2 * n] + picked[2 * n : 3 * n]
        pix_ref[n : n + 8, cols] = picked[3 * n : 3 * n + 8] + picked[3 * n + 8 : 3 * n + 16] + picked[3 * n + 16 : 3 * n + 24]
    big[0].wait()
    for t in range(pixels // lanes):
        cols = slice(t * lanes, (t + 1) * lanes)
        sine, cosine = sin_cos(phase_ref[:, cols])
        wave_ref[0:trans, cols] = cosine
        wave_ref[trans : 2 * trans, cols] = sine
    big[1].wait()
    big[2].wait()
    norms = [None, None]
    scores = [None, None]
    for step in range(blocks):
        col0 = step * chunk
        part0 = step * tiles * part_dev * 2
        refs0 = step * tiles * ori_dev * 2
        split_planes((part_dev, tiles, lambda i, t: part_ref[i, :, pl.ds(col0 + t * lanes, lanes)]), part_rows, part0)
        split_planes((ori_dev, tiles, lambda j, t: refs_ref[j, :, pl.ds(col0 + t * lanes, lanes)]), refs_rows, refs0)
        squares = []
        weighted = [[], []]
        for t in range(tiles):
            cols = slice(col0 + t * lanes, col0 + (t + 1) * lanes)
            part_r = read_plane(part_rows, part0, part_dev, t, 0)
            part_m = read_plane(part_rows, part0, part_dev, t, 1)
            refs_r = read_plane(refs_rows, refs0, ori_dev, t, 0)
            refs_m = read_plane(refs_rows, refs0, ori_dev, t, 1)
            ctf = pix_ref[0:n, cols]
            scaled_ref[0:n, cols] = part_r * ctf
            scaled_ref[n : 2 * n, cols] = part_m * ctf
            inv = jnp.concatenate([pix_ref[n : n + 8, cols]] * (ori_dev // 8), axis=0)
            for p, plane in enumerate((refs_r, refs_m)):
                weighted[p].append((plane * inv).astype(bf16))
                planes_ref[:, pl.ds(2 * col0 + p * chunk + t * lanes, lanes)] = plane.astype(bf16)
            power = jnp.concatenate([refs_r * refs_r + refs_m * refs_m, part_r * part_r + part_m * part_m], axis=0)
            high = power.astype(bf16).astype(f32)
            squares.append((high.astype(bf16), (power - high).astype(bf16)))
        for t in range(tiles):
            cols = slice(col0 + t * lanes, col0 + (t + 1) * lanes)

            def store(p, i, value):
                at = 2 * col0 + p * chunk + t * lanes
                img_ref[i * trans : (i + 1) * trans, at : at + lanes] = value

            write_images(
                store, scaled_ref, col0 + t * lanes, wave_ref[0:trans, cols], wave_ref[trans : 2 * trans, cols], n
            )
        at = 2 * col0
        more = nt(img_ref[:, at : at + chunk], jnp.concatenate(weighted[0], axis=1)) + nt(
            img_ref[:, at + chunk : at + 2 * chunk], jnp.concatenate(weighted[1], axis=1)
        )
        scores[0] = more if scores[0] is None else scores[0] + more
        for p in range(2):
            more = nt(jnp.concatenate([sq[p] for sq in squares], axis=1), hot_ref[:, col0 : col0 + chunk])
            norms[p] = more if norms[p] is None else norms[p] + more
    scores = scores[0]

    both = ori_dev + part_dev
    norms = norms[0] + norms[1]
    ref_norm = norms[0:ori_dev]
    part_norm = norms[ori_dev:both]
    ctf_square = ctf_rows * ctf_rows
    energy = ref_norm / sigma
    quadratic = 0.5 * nt(ctf_square, energy, precision=highest)
    allowed = jnp.where(mask_ref[...] == 1, 1.0, 0.0)
    wide = (part_dev, trans, ori_dev)
    scores = scores.reshape(wide) - jnp.broadcast_to(quadratic[:, None, :], wide)
    scores = jnp.where(jnp.broadcast_to(allowed[:, None, :], wide) > 0.5, scores, -1e30)
    peak = jnp.max(jnp.max(scores, axis=1, keepdims=True), axis=2, keepdims=True)
    e = jnp.exp(scores - peak)
    orient_sums = jnp.sum(e, axis=1)
    e_wide = e.reshape(pairs, ori_dev)
    e_ref[...] = e_wide
    high = e_wide.astype(bf16)
    e_rows = jnp.concatenate([high.astype(f32), e_wide - high.astype(f32)], axis=1).astype(bf16)

    cross = None
    for step in range(blocks):
        col0 = step * chunk
        plane = planes_ref[:, 2 * col0 : 2 * (col0 + chunk)]
        mixed = nn(e_rows, jnp.concatenate([plane, plane], axis=0))
        total = None
        for p in range(2):
            at = 2 * col0 + p * chunk
            part = mixed[:, p * chunk : (p + 1) * chunk] * img_ref[:, at : at + chunk].astype(f32)
            total = part if total is None else total + part
        folded = total.reshape(part_dev, trans // 8, 8, chunk).sum(axis=1).reshape(part_dev * 8, chunk)
        folded = folded.astype(bf16)
        more = [
            nt(folded[:, k * chunk // 2 : (k + 1) * chunk // 2], hot_ref[:, col0 + k * chunk // 2 : col0 + (k + 1) * chunk // 2])
            for k in range(2)
        ]
        cross = more if cross is None else [old + new for old, new in zip(cross, more)]
    cross = (cross[0] + cross[1]).reshape(part_dev, 8, shells).sum(axis=1)
    total = jnp.sum(orient_sums, axis=1, keepdims=True)
    third = ctf_square * nn(orient_sums, ref_norm, precision=highest)
    noise = part_norm * total - 2.0 * cross + third
    lane = lax.broadcasted_iota(jnp.int32, (part_dev, lanes), 1)
    stat = jnp.concatenate([noise, jnp.zeros((part_dev, lanes - shells), f32)], axis=1)
    for k, piece in enumerate(pieces(peak.reshape(part_dev, 1), 3) + pieces(total, 3)):
        stat = jnp.where(lane == shells + k, jnp.broadcast_to(piece.astype(f32), lane.shape), stat)
    message = jnp.concatenate([e_wide.T, stat], axis=0).astype(bf16)

    def spread(dest, carry):
        message_ref[dest] = message
        return carry

    lax.fori_loop(0, message_ref.shape[0], spread, 0, unroll=8)


def column_kernel(
    group_hbm,
    recv_ref,
    phase_hbm,
    shell_hbm,
    table_hbm,
    scaled_hbm,
    wave_hbm,
    square_hbm,
    group_ref,
    phase_ref,
    shell_ref,
    table_ref,
    scaled_ref,
    wave_ref,
    square_ref,
    rows_ref,
    planes_ref,
    ctf_ref,
    sems,
):
    sources, part_dev, _, width = recv_ref.shape
    trans = phase_ref.shape[0]
    shells = table_ref.shape[1]
    pairs = part_dev * trans
    tiles = width // lanes
    span = wave_tile // lanes
    start = pl.multiple_of(lax.axis_index("dom") * width, width)
    copies = start_all(
        [
            (group_hbm, group_ref),
            (table_hbm, table_ref),
            (shell_hbm.at[:, pl.ds(start, width)], shell_ref),
            (phase_hbm.at[:, pl.ds(start, width)], phase_ref),
        ],
        sems,
    )
    for copy in copies:
        copy.wait()
    for i in range(sources * part_dev):
        rows_ref[pl.ds(i, 1), :] = table_ref[pl.ds(group_ref[i], 1), :]
    hot = one_hot(shell_ref[...], shells)
    everyone = rows_ref[...]
    ctf_ref[...] = sum(nn(piece, hot) for piece in pieces(everyone, 3))
    for t in range(tiles):
        at = (t // span * 2 * span + t % span) * lanes
        sine, cosine = sin_cos(phase_ref[:, pl.ds(t * lanes, lanes)])
        for wave, offset in ((cosine, at), (sine, at + wave_tile)):
            high = wave.astype(bf16)
            wave_ref[0:trans, pl.ds(offset, lanes)] = high
            wave_ref[trans : 2 * trans, pl.ds(offset, lanes)] = (wave - high.astype(f32)).astype(bf16)
    square = everyone * everyone
    high = square.astype(bf16).astype(f32)
    squares = jnp.concatenate([high, square - high], axis=1)
    square_ref[...] = (
        jnp.broadcast_to(squares[:, None, :], (sources * part_dev, trans, 2 * shells))
        .reshape(sources * pairs, 2 * shells)
        .astype(bf16)
    )
    n = part_dev

    def source_step(src, carry):
        plane0 = pl.multiple_of(src * (tiles * part_dev * 2), tiles * part_dev * 2)
        split_planes((part_dev, tiles, lambda i, t: recv_ref[src, i, :, pl.ds(t * lanes, lanes)]), planes_ref, plane0)
        rows = pl.ds(pl.multiple_of(src * n, n), n)
        for t in range(tiles):
            cols = pl.ds(t * lanes, lanes)
            ctf = ctf_ref[rows, cols]
            for p in range(2):
                scaled_ref[p, rows, cols] = read_plane(planes_ref, plane0, part_dev, t, p) * ctf
        return carry

    lax.fori_loop(0, sources, source_step, 0, unroll=2)
    copies = start_all([(scaled_ref, scaled_hbm), (wave_ref, wave_hbm), (square_ref, square_hbm)], sems)
    for copy in copies:
        copy.wait()


def sum_kernel(
    orients,
    shells,
    scale,
    scaled_hbm,
    wave_hbm,
    square_hbm,
    recv_ref,
    e_ref,
    post_ref,
    sums_ref,
    weights_ref,
    noise_ref,
    scaled_ref,
    wave_ref,
    square_ref,
    half_ref,
    left_ref,
    share_ref,
    sems,
):
    pairs, ori_dev = e_ref.shape
    part_dev = recv_ref.shape[1] - ori_dev
    trans = pairs // part_dev
    sources = recv_ref.shape[0] // orients
    copies = start_all([(wave_hbm, wave_ref), (scaled_hbm, scaled_ref), (square_hbm, square_ref)], sems)
    me = lax.axis_index("dom")
    mine = lax.axis_index("orient")
    lane_part = lax.broadcasted_iota(jnp.int32, (part_dev, pairs), 1) // trans
    own = lane_part == lax.broadcasted_iota(jnp.int32, (part_dev, pairs), 0)
    lane = lax.broadcasted_iota(jnp.int32, (ori_dev, pairs), 1)
    lower = lane < pairs // 2
    half_part = lane % (pairs // 2) // trans
    row = lax.broadcasted_iota(jnp.int32, (lanes, 2 * lanes), 0) - shells
    upper = lax.broadcasted_iota(jnp.int32, (lanes, 2 * lanes), 1) // lanes
    picker = jnp.where((row >= 3 * upper) & (row < 3 * upper + 3), 1.0, 0.0).astype(bf16)

    stats = recv_ref[:, ori_dev : ori_dev + part_dev, :].astype(f32)
    rows = stats.reshape(sources * orients * part_dev, lanes).astype(bf16)
    decoded = nn(rows, picker)
    shape = (sources, orients, part_dev, lanes)
    peaks = decoded[:, 0:lanes].reshape(shape)
    totals = decoded[:, lanes : 2 * lanes].reshape(shape)
    shares = jnp.exp(peaks - jnp.max(peaks, axis=1, keepdims=True))
    shares = shares * (1.0 / jnp.sum(shares * totals, axis=1, keepdims=True))
    noise = jnp.sum(shares * stats.reshape(shape), axis=(0, 1))
    noise_ref[...] = jnp.sum(noise, axis=0, keepdims=True)[:, 0:shells] * scale
    share_ref[...] = shares.reshape(sources * orients, part_dev, lanes)
    for src in range(sources):
        factor = share_ref[src * orients + mine]
        lane = jnp.sum(jnp.where(own, factor, 0.0), axis=0, keepdims=True)
        post = recv_ref[src * orients + mine, 0:ori_dev, :].astype(f32) * lane
        high = post.astype(bf16).astype(f32)
        low = post - high
        half_ref[:, pl.ds(src * pairs, pairs)] = jnp.concatenate([high, low], axis=0).astype(bf16)
        turned = [pltpu.roll(x, pairs // 2, 1) for x in (high, low)]
        mixes = (jnp.where(lower, high, turned[1]), jnp.where(lower, turned[0], low))
        highs = (high, turned[0])
        for i in range(part_dev):
            rows = pl.ds((src * part_dev + i) * ori_dev, ori_dev)
            group = i // (part_dev // 2)
            here = half_part == i % (part_dev // 2)
            left_ref[rows, 0:pairs] = jnp.where(here, mixes[group], 0.0).astype(bf16)
            left_ref[rows, pairs : 2 * pairs] = jnp.where(here & lower, highs[group], 0.0).astype(bf16)
    factor = share_ref[me * orients + mine][:, 0:ori_dev]
    wide = (part_dev, trans, ori_dev)
    post_ref[...] = (e_ref[...].reshape(wide) * jnp.broadcast_to(factor[:, None, :], wide)).reshape(pairs, ori_dev)
    copies[0].wait()
    copies[1].wait()
    for tile in range(sums_ref.shape[2] // wave_tile):
        cols = slice(tile * wave_tile, (tile + 1) * wave_tile)
        waves = wave_ref[:, 2 * tile * wave_tile : 2 * (tile + 1) * wave_tile]
        high = waves[0:trans]
        low = waves[trans : 2 * trans]
        mixed = nn(left_ref[...], jnp.concatenate([high] * part_dev + [low] * part_dev, axis=0))
        sums = [None, None]
        for i in range(sources * part_dev):
            block = mixed[i * ori_dev : (i + 1) * ori_dev]
            cosine = block[:, 0:wave_tile]
            sine = block[:, wave_tile : 2 * wave_tile]
            r = jnp.broadcast_to(scaled_ref[0, i : i + 1, cols], cosine.shape)
            m = jnp.broadcast_to(scaled_ref[1, i : i + 1, cols], cosine.shape)
            more = (r * cosine - m * sine, r * sine + m * cosine)
            sums = [new if old is None else old + new for old, new in zip(sums, more)]
        for p in range(2):
            for j in range(ori_dev):
                sums_ref[j, p : p + 1, cols] = sums[p][j : j + 1, :]
    copies[2].wait()
    weights = nn(half_ref[...], square_ref[...])
    weights = weights[0:ori_dev] + weights[ori_dev : 2 * ori_dev]
    weights_ref[...] = weights[:, 0:shells] + weights[:, shells : 2 * shells]


def on_device(particles, references, phases, mask, ctf_group, ctf_table, shell_index, sigma2):
    part_dev, _, pixels = particles.shape
    ori_dev = references.shape[0]
    trans = phases.shape[0]
    shells = ctf_table.shape[1]
    dom = lax.axis_size("dom")
    orients = lax.axis_size("orient")
    width = pixels // dom
    pairs = part_dev * trans
    chunk = 4096
    shell_row = shell_index.reshape(1, pixels)
    sigma_row = sigma2.reshape(1, shells)
    vmem = pl.BlockSpec(memory_space=pltpu.VMEM)
    smem = pl.BlockSpec(memory_space=pltpu.SMEM)
    anywhere = pl.BlockSpec(memory_space=pl.ANY)
    params = pltpu.CompilerParams(vmem_limit_bytes=20 * 1024 * 1024)
    far = lambda x: pltpu.with_memory_space_constraint(x, pltpu.HBM)
    dma = pltpu.SemaphoreType.DMA

    send = pl.pallas_call(
        pack_kernel,
        out_shape=pltpu.VMEM((dom, part_dev, 2, width), bf16),
        in_specs=[anywhere],
        out_specs=vmem,
        scratch_shapes=[dma((dom,))],
        compiler_params=params,
        name="pack",
    )(far(particles))
    recv = lax.all_to_all(send, "dom", 0, 0)

    both = ori_dev + part_dev
    message, e = pl.pallas_call(
        functools.partial(score_kernel, chunk),
        out_shape=(
            pltpu.VMEM((dom * orients, both, lanes), bf16),
            jax.ShapeDtypeStruct((pairs, ori_dev), f32),
        ),
        in_specs=[anywhere] * 8,
        out_specs=(vmem, vmem),
        scratch_shapes=[
            pltpu.VMEM(particles.shape, bf16),
            pltpu.VMEM(references.shape, bf16),
            pltpu.VMEM(phases.shape, f32),
            pltpu.VMEM((1, pixels), jnp.int32),
            pltpu.VMEM(mask.shape, jnp.int32),
            pltpu.VMEM(ctf_table.shape, f32),
            pltpu.VMEM((1, shells), f32),
            pltpu.SMEM(ctf_group.shape, jnp.int32),
            pltpu.VMEM((pixels // lanes * part_dev * 2, lanes), f32),
            pltpu.VMEM((pixels // lanes * ori_dev * 2, lanes), f32),
            pltpu.VMEM((pairs, 2 * pixels), bf16),
            pltpu.VMEM((ori_dev, 2 * pixels), bf16),
            pltpu.VMEM((shells, pixels), bf16),
            pltpu.VMEM((2 * part_dev, pixels), f32),
            pltpu.VMEM((part_dev + 8, pixels), f32),
            pltpu.VMEM((2 * trans, pixels), f32),
            pltpu.VMEM((part_dev, shells), f32),
            dma((5,)),
            dma((3,)),
        ],
        compiler_params=params,
        name="scores",
    )(
        far(ctf_group),
        far(particles),
        far(references),
        far(phases),
        far(shell_row),
        far(mask),
        far(ctf_table),
        far(sigma_row),
    )

    messages = lax.all_to_all(message, ("dom", "orient"), 0, 0)

    particles_all = dom * part_dev
    columns = (
        ((2, particles_all, width), f32),
        ((2 * trans, 2 * width), bf16),
        ((particles_all * trans, 2 * shells), bf16),
    )
    scaled, waves, squares = pl.pallas_call(
        column_kernel,
        out_shape=tuple(pltpu.HBM(*column) for column in columns),
        in_specs=[anywhere, vmem] + [anywhere] * 3,
        out_specs=(anywhere,) * 3,
        scratch_shapes=[
            pltpu.SMEM(ctf_group.shape, jnp.int32),
            pltpu.VMEM((trans, width), f32),
            pltpu.VMEM((1, width), jnp.int32),
            pltpu.VMEM(ctf_table.shape, f32),
        ]
        + [pltpu.VMEM(*column) for column in columns]
        + [
            pltpu.VMEM((particles_all, shells), f32),
            pltpu.VMEM((particles_all * 2 * width // lanes, lanes), f32),
            pltpu.VMEM((particles_all, width), f32),
            dma((4,)),
        ],
        compiler_params=params,
        name="columns",
    )(far(ctf_group), recv, far(phases), far(shell_row), far(ctf_table))

    scale = shells / (part_dev * dom * pixels)
    posterior, image_sums, ctf_weights, noise = pl.pallas_call(
        functools.partial(sum_kernel, orients, shells, scale),
        out_shape=(
            jax.ShapeDtypeStruct((pairs, ori_dev), f32),
            jax.ShapeDtypeStruct((ori_dev, 2, width), f32),
            jax.ShapeDtypeStruct((ori_dev, shells), f32),
            jax.ShapeDtypeStruct((1, shells), f32),
        ),
        in_specs=[anywhere, anywhere, anywhere, vmem, vmem],
        out_specs=(vmem, vmem, vmem, vmem),
        scratch_shapes=[pltpu.VMEM(*column) for column in columns]
        + [
            pltpu.VMEM((2 * ori_dev, particles_all * trans), bf16),
            pltpu.VMEM((particles_all * ori_dev, 2 * pairs), bf16),
            pltpu.VMEM((dom * orients, part_dev, lanes), f32),
            dma((3,)),
        ],
        compiler_params=params,
        name="sums",
    )(far(scaled), far(waves), far(squares), messages, e)
    return (
        posterior.reshape(part_dev, trans, ori_dev),
        image_sums,
        ctf_weights,
        noise.reshape(shells),
    )


def solution(mesh):
    return jax.shard_map(
        on_device,
        mesh=mesh,
        in_specs=(
            P("dom", None, None),
            P("orient", None, None),
            P(),
            P("dom", "orient"),
            P(),
            P(),
            P(),
            P(),
        ),
        out_specs=(P("dom", None, "orient"), P("orient", None, "dom"), P("orient", None), P()),
        check_vma=False,
    )
```

```python
import functools

import jax
import jax.numpy as jnp
from jax import lax
from jax.experimental import pallas as pl
from jax.experimental.pallas import tpu as pltpu
from jax.sharding import PartitionSpec as P

f32 = jnp.float32
bf16 = jnp.bfloat16
highest = lax.Precision.HIGHEST
lanes = 128
wave_tile = 256

sin_terms = (0.9999999766, -0.1666664762, 0.008332899654, -0.000198008873, 2.590467297e-06)
cos_terms = (0.9999999998, -0.4999999936, 0.04166663624, -0.001388836119, 2.47601506e-05, -2.605130157e-07)


def horner(terms, z):
    total = terms[-1] * z + terms[-2]
    for term in terms[-3::-1]:
        total = total * z + term
    return total


def sin_cos(angle):
    half = angle * 0.5
    z = half * half
    s = half * horner(sin_terms, z)
    c = horner(cos_terms, z)
    twice = s + s
    return twice * c, 1.0 - twice * s


def pieces(x, count):
    out = []
    rest = x
    for step in range(count):
        piece = rest.astype(bf16)
        out.append(piece)
        if step + 1 < count:
            rest = rest - piece.astype(f32)
    return out


def nt(a, b, **kw):
    return lax.dot_general(a, b, (((1,), (1,)), ((), ())), preferred_element_type=f32, **kw)


def tn(a, b, **kw):
    return lax.dot_general(a, b, (((0,), (0,)), ((), ())), preferred_element_type=f32, **kw)


def nn(a, b, **kw):
    return lax.dot_general(a, b, (((1,), (0,)), ((), ())), preferred_element_type=f32, **kw)


def one_hot(index_row, shells):
    rows = lax.broadcasted_iota(jnp.int32, (shells, index_row.shape[1]), 0)
    return jnp.where(rows == index_row, 1.0, 0.0).astype(bf16)


def start_all(pairs, sems):
    copies = [pltpu.make_async_copy(src, dst, sems.at[k]) for k, (src, dst) in enumerate(pairs)]
    for copy in copies:
        copy.start()
    return copies


def split_planes(src, dst_ref, row0):
    items, tiles, load = src
    for tile in range(tiles):
        for item in range(items):
            dst_ref[pl.ds(row0 + (tile * items + item) * 2, 2), :] = load(item, tile).astype(f32)


def read_plane(ref, row0, items, tile, plane):
    return ref[pl.ds(row0 + tile * items * 2 + plane, items, 2), :]


def write_images(store, scaled_ref, scaled_col, cosine, sine, count):
    trans = cosine.shape[0]
    cols = pl.ds(scaled_col, lanes)
    for i in range(count):
        r = jnp.broadcast_to(scaled_ref[i : i + 1, cols], (trans, lanes))
        m = jnp.broadcast_to(scaled_ref[count + i : count + i + 1, cols], (trans, lanes))
        store(0, i, (r * cosine - m * sine).astype(bf16))
        store(1, i, (r * sine + m * cosine).astype(bf16))


def pack_kernel(part_hbm, out_ref, sems):
    dests, _, _, width = out_ref.shape
    copies = start_all(
        [(part_hbm.at[:, :, pl.ds(dest * width, width)], out_ref.at[dest]) for dest in range(dests)], sems
    )
    for copy in copies:
        copy.wait()


def score_kernel(
    chunk,
    group_hbm,
    part_hbm,
    refs_hbm,
    phase_hbm,
    shell_hbm,
    mask_hbm,
    table_hbm,
    sigma_hbm,
    message_ref,
    e_ref,
    part_ref,
    refs_ref,
    phase_ref,
    shell_ref,
    mask_ref,
    table_ref,
    sigma_ref,
    group_ref,
    part_rows,
    refs_rows,
    img_ref,
    planes_ref,
    hot_ref,
    scaled_ref,
    pix_ref,
    wave_ref,
    rows_ref,
    small_sems,
    big_sems,
):
    part_dev, _, pixels = part_ref.shape
    ori_dev = refs_ref.shape[0]
    trans = phase_ref.shape[0]
    shells = table_ref.shape[1]
    pairs = part_dev * trans
    blocks = pixels // chunk
    tiles = chunk // lanes
    first = lax.axis_index("dom") * part_dev
    small = start_all(
        [
            (group_hbm, group_ref),
            (table_hbm, table_ref),
            (sigma_hbm, sigma_ref),
            (shell_hbm, shell_ref),
            (mask_hbm, mask_ref),
        ],
        small_sems,
    )
    big = start_all([(phase_hbm, phase_ref), (part_hbm, part_ref), (refs_hbm, refs_ref)], big_sems)
    for copy in small:
        copy.wait()

    for i in range(part_dev):
        rows_ref[pl.ds(i, 1), :] = table_ref[pl.ds(group_ref[first + i], 1), :]
    ctf_rows = rows_ref[...]
    sigma = sigma_ref[...]
    inverse = jnp.broadcast_to(1.0 / sigma, (8, shells))
    table = jnp.concatenate(
        [p.astype(f32) for p in pieces(ctf_rows, 3)] + [p.astype(f32) for p in pieces(inverse, 3)], axis=0
    ).astype(bf16)
    n = part_dev
    for step in range(blocks):
        cols = slice(step * chunk, (step + 1) * chunk)
        hot = one_hot(shell_ref[:, cols], shells)
        hot_ref[:, cols] = hot
        picked = nn(table, hot)
        pix_ref[0:n, cols] = picked[0:n] + picked[n : 2 * n] + picked[2 * n : 3 * n]
        pix_ref[n : n + 8, cols] = picked[3 * n : 3 * n + 8] + picked[3 * n + 8 : 3 * n + 16] + picked[3 * n + 16 : 3 * n + 24]
    big[0].wait()
    for t in range(pixels // lanes):
        cols = slice(t * lanes, (t + 1) * lanes)
        sine, cosine = sin_cos(phase_ref[:, cols])
        wave_ref[0:trans, cols] = cosine
        wave_ref[trans : 2 * trans, cols] = sine
    big[1].wait()
    big[2].wait()
    norms = [None, None]
    scores = [None, None]
    for step in range(blocks):
        col0 = step * chunk
        part0 = step * tiles * part_dev * 2
        refs0 = step * tiles * ori_dev * 2
        split_planes((part_dev, tiles, lambda i, t: part_ref[i, :, pl.ds(col0 + t * lanes, lanes)]), part_rows, part0)
        split_planes((ori_dev, tiles, lambda j, t: refs_ref[j, :, pl.ds(col0 + t * lanes, lanes)]), refs_rows, refs0)
        squares = []
        weighted = [[], []]
        for t in range(tiles):
            cols = slice(col0 + t * lanes, col0 + (t + 1) * lanes)
            part_r = read_plane(part_rows, part0, part_dev, t, 0)
            part_m = read_plane(part_rows, part0, part_dev, t, 1)
            refs_r = read_plane(refs_rows, refs0, ori_dev, t, 0)
            refs_m = read_plane(refs_rows, refs0, ori_dev, t, 1)
            ctf = pix_ref[0:n, cols]
            scaled_ref[0:n, cols] = part_r * ctf
            scaled_ref[n : 2 * n, cols] = part_m * ctf
            inv = jnp.concatenate([pix_ref[n : n + 8, cols]] * (ori_dev // 8), axis=0)
            for p, plane in enumerate((refs_r, refs_m)):
                weighted[p].append((plane * inv).astype(bf16))
                planes_ref[:, pl.ds(2 * col0 + p * chunk + t * lanes, lanes)] = plane.astype(bf16)
            power = jnp.concatenate([refs_r * refs_r + refs_m * refs_m, part_r * part_r + part_m * part_m], axis=0)
            high = power.astype(bf16).astype(f32)
            squares.append((high.astype(bf16), (power - high).astype(bf16)))
        for t in range(tiles):
            cols = slice(col0 + t * lanes, col0 + (t + 1) * lanes)

            def store(p, i, value):
                at = 2 * col0 + p * chunk + t * lanes
                img_ref[i * trans : (i + 1) * trans, at : at + lanes] = value

            write_images(
                store, scaled_ref, col0 + t * lanes, wave_ref[0:trans, cols], wave_ref[trans : 2 * trans, cols], n
            )
        at = 2 * col0
        more = nt(img_ref[:, at : at + chunk], jnp.concatenate(weighted[0], axis=1)) + nt(
            img_ref[:, at + chunk : at + 2 * chunk], jnp.concatenate(weighted[1], axis=1)
        )
        scores[0] = more if scores[0] is None else scores[0] + more
        for p in range(2):
            more = nt(jnp.concatenate([sq[p] for sq in squares], axis=1), hot_ref[:, col0 : col0 + chunk])
            norms[p] = more if norms[p] is None else norms[p] + more
    scores = scores[0]

    both = ori_dev + part_dev
    norms = norms[0] + norms[1]
    ref_norm = norms[0:ori_dev]
    part_norm = norms[ori_dev:both]
    ctf_square = ctf_rows * ctf_rows
    energy = ref_norm / sigma
    quadratic = 0.5 * nt(ctf_square, energy, precision=highest)
    allowed = jnp.where(mask_ref[...] == 1, 1.0, 0.0)
    wide = (part_dev, trans, ori_dev)
    scores = scores.reshape(wide) - jnp.broadcast_to(quadratic[:, None, :], wide)
    scores = jnp.where(jnp.broadcast_to(allowed[:, None, :], wide) > 0.5, scores, -1e30)
    peak = jnp.max(jnp.max(scores, axis=1, keepdims=True), axis=2, keepdims=True)
    e = jnp.exp(scores - peak)
    orient_sums = jnp.sum(e, axis=1)
    e_wide = e.reshape(pairs, ori_dev)
    e_ref[...] = e_wide
    high = e_wide.astype(bf16)
    e_rows = jnp.concatenate([high.astype(f32), e_wide - high.astype(f32)], axis=1).astype(bf16)

    cross = None
    for step in range(blocks):
        col0 = step * chunk
        plane = planes_ref[:, 2 * col0 : 2 * (col0 + chunk)]
        mixed = nn(e_rows, jnp.concatenate([plane, plane], axis=0))
        total = None
        for p in range(2):
            at = 2 * col0 + p * chunk
            part = mixed[:, p * chunk : (p + 1) * chunk] * img_ref[:, at : at + chunk].astype(f32)
            total = part if total is None else total + part
        folded = total.reshape(part_dev, trans // 8, 8, chunk).sum(axis=1).reshape(part_dev * 8, chunk)
        folded = folded.astype(bf16)
        more = [
            nt(folded[:, k * chunk // 2 : (k + 1) * chunk // 2], hot_ref[:, col0 + k * chunk // 2 : col0 + (k + 1) * chunk // 2])
            for k in range(2)
        ]
        cross = more if cross is None else [old + new for old, new in zip(cross, more)]
    cross = (cross[0] + cross[1]).reshape(part_dev, 8, shells).sum(axis=1)
    total = jnp.sum(orient_sums, axis=1, keepdims=True)
    third = ctf_square * nn(orient_sums, ref_norm, precision=highest)
    noise = part_norm * total - 2.0 * cross + third
    lane = lax.broadcasted_iota(jnp.int32, (part_dev, lanes), 1)
    stat = jnp.concatenate([noise, jnp.zeros((part_dev, lanes - shells), f32)], axis=1)
    for k, piece in enumerate(pieces(peak.reshape(part_dev, 1), 3) + pieces(total, 3)):
        stat = jnp.where(lane == shells + k, jnp.broadcast_to(piece.astype(f32), lane.shape), stat)
    message = jnp.concatenate([e_wide.T, stat], axis=0).astype(bf16)

    def spread(dest, carry):
        message_ref[dest] = message
        return carry

    lax.fori_loop(0, message_ref.shape[0], spread, 0, unroll=8)


def column_kernel(
    group_hbm,
    recv_ref,
    phase_hbm,
    shell_hbm,
    table_hbm,
    scaled_ref,
    wave_ref,
    square_hbm,
    group_ref,
    phase_ref,
    shell_ref,
    table_ref,
    square_ref,
    rows_ref,
    planes_ref,
    ctf_ref,
    sems,
):
    sources, part_dev, _, width = recv_ref.shape
    trans = phase_ref.shape[0]
    shells = table_ref.shape[1]
    pairs = part_dev * trans
    tiles = width // lanes
    span = wave_tile // lanes
    start = pl.multiple_of(lax.axis_index("dom") * width, width)
    copies = start_all(
        [
            (group_hbm, group_ref),
            (table_hbm, table_ref),
            (shell_hbm.at[:, pl.ds(start, width)], shell_ref),
            (phase_hbm.at[:, pl.ds(start, width)], phase_ref),
        ],
        sems,
    )
    for copy in copies:
        copy.wait()
    for i in range(sources * part_dev):
        rows_ref[pl.ds(i, 1), :] = table_ref[pl.ds(group_ref[i], 1), :]
    hot = one_hot(shell_ref[...], shells)
    everyone = rows_ref[...]
    ctf_ref[...] = sum(nn(piece, hot) for piece in pieces(everyone, 3))
    for t in range(tiles):
        at = (t // span * 2 * span + t % span) * lanes
        sine, cosine = sin_cos(phase_ref[:, pl.ds(t * lanes, lanes)])
        for wave, offset in ((cosine, at), (sine, at + wave_tile)):
            high = wave.astype(bf16)
            wave_ref[0:trans, pl.ds(offset, lanes)] = high
            wave_ref[trans : 2 * trans, pl.ds(offset, lanes)] = (wave - high.astype(f32)).astype(bf16)
    square = everyone * everyone
    high = square.astype(bf16).astype(f32)
    squares = jnp.concatenate([high, square - high], axis=1)
    square_ref[...] = (
        jnp.broadcast_to(squares[:, None, :], (sources * part_dev, trans, 2 * shells))
        .reshape(sources * pairs, 2 * shells)
        .astype(bf16)
    )
    square_copy = pltpu.make_async_copy(square_ref, square_hbm, sems.at[0])
    square_copy.start()
    n = part_dev

    def source_step(src, carry):
        plane0 = pl.multiple_of(src * (tiles * part_dev * 2), tiles * part_dev * 2)
        split_planes((part_dev, tiles, lambda i, t: recv_ref[src, i, :, pl.ds(t * lanes, lanes)]), planes_ref, plane0)
        rows = pl.ds(pl.multiple_of(src * n, n), n)
        for t in range(tiles):
            cols = pl.ds(t * lanes, lanes)
            ctf = ctf_ref[rows, cols]
            for p in range(2):
                scaled_ref[p, rows, cols] = read_plane(planes_ref, plane0, part_dev, t, p) * ctf
        return carry

    lax.fori_loop(0, sources, source_step, 0, unroll=2)
    square_copy.wait()


def sum_kernel(
    orients,
    shells,
    scale,
    scaled_ref,
    wave_ref,
    square_hbm,
    recv_ref,
    e_ref,
    post_ref,
    sums_ref,
    weights_ref,
    noise_ref,
    square_ref,
    half_ref,
    left_ref,
    share_ref,
    sem,
):
    pairs, ori_dev = e_ref.shape
    part_dev = recv_ref.shape[1] - ori_dev
    trans = pairs // part_dev
    sources = recv_ref.shape[0] // orients
    square_copy = pltpu.make_async_copy(square_hbm, square_ref, sem)
    square_copy.start()
    me = lax.axis_index("dom")
    mine = lax.axis_index("orient")
    lane_part = lax.broadcasted_iota(jnp.int32, (part_dev, pairs), 1) // trans
    own = lane_part == lax.broadcasted_iota(jnp.int32, (part_dev, pairs), 0)
    lane = lax.broadcasted_iota(jnp.int32, (ori_dev, pairs), 1)
    lower = lane < pairs // 2
    half_part = lane % (pairs // 2) // trans
    row = lax.broadcasted_iota(jnp.int32, (lanes, 2 * lanes), 0) - shells
    upper = lax.broadcasted_iota(jnp.int32, (lanes, 2 * lanes), 1) // lanes
    picker = jnp.where((row >= 3 * upper) & (row < 3 * upper + 3), 1.0, 0.0).astype(bf16)

    stats = recv_ref[:, ori_dev : ori_dev + part_dev, :].astype(f32)
    rows = stats.reshape(sources * orients * part_dev, lanes).astype(bf16)
    decoded = nn(rows, picker)
    shape = (sources, orients, part_dev, lanes)
    peaks = decoded[:, 0:lanes].reshape(shape)
    totals = decoded[:, lanes : 2 * lanes].reshape(shape)
    shares = jnp.exp(peaks - jnp.max(peaks, axis=1, keepdims=True))
    shares = shares * (1.0 / jnp.sum(shares * totals, axis=1, keepdims=True))
    noise = jnp.sum(shares * stats.reshape(shape), axis=(0, 1))
    noise_ref[...] = jnp.sum(noise, axis=0, keepdims=True)[:, 0:shells] * scale
    share_ref[...] = shares.reshape(sources * orients, part_dev, lanes)
    for src in range(sources):
        factor = share_ref[src * orients + mine]
        lane = jnp.sum(jnp.where(own, factor, 0.0), axis=0, keepdims=True)
        post = recv_ref[src * orients + mine, 0:ori_dev, :].astype(f32) * lane
        high = post.astype(bf16).astype(f32)
        low = post - high
        half_ref[:, pl.ds(src * pairs, pairs)] = jnp.concatenate([high, low], axis=0).astype(bf16)
        turned = [pltpu.roll(x, pairs // 2, 1) for x in (high, low)]
        mixes = (jnp.where(lower, high, turned[1]), jnp.where(lower, turned[0], low))
        highs = (high, turned[0])
        for i in range(part_dev):
            rows = pl.ds((src * part_dev + i) * ori_dev, ori_dev)
            group = i // (part_dev // 2)
            here = half_part == i % (part_dev // 2)
            left_ref[rows, 0:pairs] = jnp.where(here, mixes[group], 0.0).astype(bf16)
            left_ref[rows, pairs : 2 * pairs] = jnp.where(here & lower, highs[group], 0.0).astype(bf16)
    factor = share_ref[me * orients + mine][:, 0:ori_dev]
    wide = (part_dev, trans, ori_dev)
    post_ref[...] = (e_ref[...].reshape(wide) * jnp.broadcast_to(factor[:, None, :], wide)).reshape(pairs, ori_dev)
    for tile in range(sums_ref.shape[2] // wave_tile):
        cols = slice(tile * wave_tile, (tile + 1) * wave_tile)
        waves = wave_ref[:, 2 * tile * wave_tile : 2 * (tile + 1) * wave_tile]
        high = waves[0:trans]
        low = waves[trans : 2 * trans]
        mixed = nn(left_ref[...], jnp.concatenate([high] * part_dev + [low] * part_dev, axis=0))
        sums = [None, None]
        for i in range(sources * part_dev):
            block = mixed[i * ori_dev : (i + 1) * ori_dev]
            cosine = block[:, 0:wave_tile]
            sine = block[:, wave_tile : 2 * wave_tile]
            r = jnp.broadcast_to(scaled_ref[0, i : i + 1, cols], cosine.shape)
            m = jnp.broadcast_to(scaled_ref[1, i : i + 1, cols], cosine.shape)
            more = (r * cosine - m * sine, r * sine + m * cosine)
            sums = [new if old is None else old + new for old, new in zip(sums, more)]
        for p in range(2):
            for j in range(ori_dev):
                sums_ref[j, p : p + 1, cols] = sums[p][j : j + 1, :]
    square_copy.wait()
    weights = nn(half_ref[...], square_ref[...])
    weights = weights[0:ori_dev] + weights[ori_dev : 2 * ori_dev]
    weights_ref[...] = weights[:, 0:shells] + weights[:, shells : 2 * shells]


def on_device(particles, references, phases, mask, ctf_group, ctf_table, shell_index, sigma2):
    part_dev, _, pixels = particles.shape
    ori_dev = references.shape[0]
    trans = phases.shape[0]
    shells = ctf_table.shape[1]
    dom = lax.axis_size("dom")
    orients = lax.axis_size("orient")
    width = pixels // dom
    pairs = part_dev * trans
    chunk = 4096
    shell_row = shell_index.reshape(1, pixels)
    sigma_row = sigma2.reshape(1, shells)
    vmem = pl.BlockSpec(memory_space=pltpu.VMEM)
    smem = pl.BlockSpec(memory_space=pltpu.SMEM)
    anywhere = pl.BlockSpec(memory_space=pl.ANY)
    params = pltpu.CompilerParams(vmem_limit_bytes=20 * 1024 * 1024)
    far = lambda x: pltpu.with_memory_space_constraint(x, pltpu.HBM)
    dma = pltpu.SemaphoreType.DMA

    send = pl.pallas_call(
        pack_kernel,
        out_shape=pltpu.VMEM((dom, part_dev, 2, width), bf16),
        in_specs=[anywhere],
        out_specs=vmem,
        scratch_shapes=[dma((dom,))],
        compiler_params=params,
        name="pack",
    )(far(particles))
    recv = lax.all_to_all(send, "dom", 0, 0)

    both = ori_dev + part_dev
    message, e = pl.pallas_call(
        functools.partial(score_kernel, chunk),
        out_shape=(
            pltpu.VMEM((dom * orients, both, lanes), bf16),
            jax.ShapeDtypeStruct((pairs, ori_dev), f32),
        ),
        in_specs=[anywhere] * 8,
        out_specs=(vmem, vmem),
        scratch_shapes=[
            pltpu.VMEM(particles.shape, bf16),
            pltpu.VMEM(references.shape, bf16),
            pltpu.VMEM(phases.shape, f32),
            pltpu.VMEM((1, pixels), jnp.int32),
            pltpu.VMEM(mask.shape, jnp.int32),
            pltpu.VMEM(ctf_table.shape, f32),
            pltpu.VMEM((1, shells), f32),
            pltpu.SMEM(ctf_group.shape, jnp.int32),
            pltpu.VMEM((pixels // lanes * part_dev * 2, lanes), f32),
            pltpu.VMEM((pixels // lanes * ori_dev * 2, lanes), f32),
            pltpu.VMEM((pairs, 2 * pixels), bf16),
            pltpu.VMEM((ori_dev, 2 * pixels), bf16),
            pltpu.VMEM((shells, pixels), bf16),
            pltpu.VMEM((2 * part_dev, pixels), f32),
            pltpu.VMEM((part_dev + 8, pixels), f32),
            pltpu.VMEM((2 * trans, pixels), f32),
            pltpu.VMEM((part_dev, shells), f32),
            dma((5,)),
            dma((3,)),
        ],
        compiler_params=params,
        name="scores",
    )(
        far(ctf_group),
        far(particles),
        far(references),
        far(phases),
        far(shell_row),
        far(mask),
        far(ctf_table),
        far(sigma_row),
    )

    messages = lax.all_to_all(message, ("dom", "orient"), 0, 0)

    particles_all = dom * part_dev
    columns = (
        ((2, particles_all, width), f32),
        ((2 * trans, 2 * width), bf16),
        ((particles_all * trans, 2 * shells), bf16),
    )
    scaled, waves, squares = pl.pallas_call(
        column_kernel,
        out_shape=(pltpu.VMEM(*columns[0]), pltpu.VMEM(*columns[1]), pltpu.HBM(*columns[2])),
        in_specs=[anywhere, vmem] + [anywhere] * 3,
        out_specs=(vmem, vmem, anywhere),
        scratch_shapes=[
            pltpu.SMEM(ctf_group.shape, jnp.int32),
            pltpu.VMEM((trans, width), f32),
            pltpu.VMEM((1, width), jnp.int32),
            pltpu.VMEM(ctf_table.shape, f32),
        ]
        + [
            pltpu.VMEM(*columns[2]),
            pltpu.VMEM((particles_all, shells), f32),
            pltpu.VMEM((particles_all * 2 * width // lanes, lanes), f32),
            pltpu.VMEM((particles_all, width), f32),
            dma((4,)),
        ],
        compiler_params=params,
        name="columns",
    )(far(ctf_group), recv, far(phases), far(shell_row), far(ctf_table))

    scale = shells / (part_dev * dom * pixels)
    posterior, image_sums, ctf_weights, noise = pl.pallas_call(
        functools.partial(sum_kernel, orients, shells, scale),
        out_shape=(
            jax.ShapeDtypeStruct((pairs, ori_dev), f32),
            jax.ShapeDtypeStruct((ori_dev, 2, width), f32),
            jax.ShapeDtypeStruct((ori_dev, shells), f32),
            jax.ShapeDtypeStruct((1, shells), f32),
        ),
        in_specs=[vmem, vmem, anywhere, vmem, vmem],
        out_specs=(vmem, vmem, vmem, vmem),
        scratch_shapes=[
            pltpu.VMEM(*columns[2]),
            pltpu.VMEM((2 * ori_dev, particles_all * trans), bf16),
            pltpu.VMEM((particles_all * ori_dev, 2 * pairs), bf16),
            pltpu.VMEM((dom * orients, part_dev, lanes), f32),
            dma,
        ],
        compiler_params=params,
        name="sums",
    )(scaled, waves, far(squares), messages, e)
    return (
        posterior.reshape(part_dev, trans, ori_dev),
        image_sums,
        ctf_weights,
        noise.reshape(shells),
    )


def solution(mesh):
    return jax.shard_map(
        on_device,
        mesh=mesh,
        in_specs=(
            P("dom", None, None),
            P("orient", None, None),
            P(),
            P("dom", "orient"),
            P(),
            P(),
            P(),
            P(),
        ),
        out_specs=(P("dom", None, "orient"), P("orient", None, "dom"), P("orient", None), P()),
        check_vma=False,
    )
```

```python
import functools

import jax
import jax.numpy as jnp
from jax import lax
from jax.experimental import pallas as pl
from jax.experimental.pallas import tpu as pltpu
from jax.sharding import PartitionSpec as P

f32 = jnp.float32
bf16 = jnp.bfloat16
highest = lax.Precision.HIGHEST
lanes = 128
wave_tile = 256

sin_terms = (0.9999999766, -0.1666664762, 0.008332899654, -0.000198008873, 2.590467297e-06)
cos_terms = (0.9999999998, -0.4999999936, 0.04166663624, -0.001388836119, 2.47601506e-05, -2.605130157e-07)


def horner(terms, z):
    total = terms[-1] * z + terms[-2]
    for term in terms[-3::-1]:
        total = total * z + term
    return total


def sin_cos(angle):
    half = angle * 0.5
    z = half * half
    s = half * horner(sin_terms, z)
    c = horner(cos_terms, z)
    twice = s + s
    return twice * c, 1.0 - twice * s


def pieces(x, count):
    out = []
    rest = x
    for step in range(count):
        piece = rest.astype(bf16)
        out.append(piece)
        if step + 1 < count:
            rest = rest - piece.astype(f32)
    return out


def nt(a, b, **kw):
    return lax.dot_general(a, b, (((1,), (1,)), ((), ())), preferred_element_type=f32, **kw)


def tn(a, b, **kw):
    return lax.dot_general(a, b, (((0,), (0,)), ((), ())), preferred_element_type=f32, **kw)


def nn(a, b, **kw):
    return lax.dot_general(a, b, (((1,), (0,)), ((), ())), preferred_element_type=f32, **kw)


def one_hot(index_row, shells):
    rows = lax.broadcasted_iota(jnp.int32, (shells, index_row.shape[1]), 0)
    return jnp.where(rows == index_row, 1.0, 0.0).astype(bf16)


def start_all(pairs, sems):
    copies = [pltpu.make_async_copy(src, dst, sems.at[k]) for k, (src, dst) in enumerate(pairs)]
    for copy in copies:
        copy.start()
    return copies


def split_planes(src, dst_ref, row0):
    items, tiles, load = src
    for tile in range(tiles):
        for item in range(items):
            dst_ref[pl.ds(row0 + (tile * items + item) * 2, 2), :] = load(item, tile).astype(f32)


def read_plane(ref, row0, items, tile, plane):
    return ref[pl.ds(row0 + tile * items * 2 + plane, items, 2), :]


def write_images(store, scaled_ref, scaled_col, cosine, sine, count):
    trans = cosine.shape[0]
    cols = pl.ds(scaled_col, lanes)
    for i in range(count):
        r = jnp.broadcast_to(scaled_ref[i : i + 1, cols], (trans, lanes))
        m = jnp.broadcast_to(scaled_ref[count + i : count + i + 1, cols], (trans, lanes))
        store(0, i, (r * cosine - m * sine).astype(bf16))
        store(1, i, (r * sine + m * cosine).astype(bf16))


def pack_kernel(part_hbm, out_ref, sems):
    dests, _, _, width = out_ref.shape
    copies = start_all(
        [(part_hbm.at[:, :, pl.ds(dest * width, width)], out_ref.at[dest]) for dest in range(dests)], sems
    )
    for copy in copies:
        copy.wait()


def score_kernel(
    chunk,
    group_hbm,
    part_hbm,
    refs_hbm,
    phase_hbm,
    shell_hbm,
    mask_hbm,
    table_hbm,
    sigma_hbm,
    message_ref,
    e_ref,
    part_ref,
    refs_ref,
    phase_ref,
    shell_ref,
    mask_ref,
    table_ref,
    sigma_ref,
    group_ref,
    part_rows,
    refs_rows,
    img_ref,
    planes_ref,
    hot_ref,
    scaled_ref,
    pix_ref,
    wave_ref,
    rows_ref,
    small_sems,
    big_sems,
):
    part_dev, _, pixels = part_ref.shape
    ori_dev = refs_ref.shape[0]
    trans = phase_ref.shape[0]
    shells = table_ref.shape[1]
    pairs = part_dev * trans
    blocks = pixels // chunk
    tiles = chunk // lanes
    first = lax.axis_index("dom") * part_dev
    small = start_all(
        [
            (group_hbm, group_ref),
            (table_hbm, table_ref),
            (sigma_hbm, sigma_ref),
            (shell_hbm, shell_ref),
            (mask_hbm, mask_ref),
        ],
        small_sems,
    )
    big = start_all([(phase_hbm, phase_ref), (part_hbm, part_ref), (refs_hbm, refs_ref)], big_sems)
    for copy in small:
        copy.wait()

    for i in range(part_dev):
        rows_ref[pl.ds(i, 1), :] = table_ref[pl.ds(group_ref[first + i], 1), :]
    ctf_rows = rows_ref[...]
    sigma = sigma_ref[...]
    inverse = jnp.broadcast_to(1.0 / sigma, (8, shells))
    table = jnp.concatenate(
        [p.astype(f32) for p in pieces(ctf_rows, 3)] + [p.astype(f32) for p in pieces(inverse, 3)], axis=0
    ).astype(bf16)
    n = part_dev
    for step in range(blocks):
        cols = slice(step * chunk, (step + 1) * chunk)
        hot = one_hot(shell_ref[:, cols], shells)
        hot_ref[:, cols] = hot
        picked = nn(table, hot)
        pix_ref[0:n, cols] = picked[0:n] + picked[n : 2 * n] + picked[2 * n : 3 * n]
        pix_ref[n : n + 8, cols] = picked[3 * n : 3 * n + 8] + picked[3 * n + 8 : 3 * n + 16] + picked[3 * n + 16 : 3 * n + 24]
    big[0].wait()
    for t in range(pixels // lanes):
        cols = slice(t * lanes, (t + 1) * lanes)
        sine, cosine = sin_cos(phase_ref[:, cols])
        wave_ref[0:trans, cols] = cosine
        wave_ref[trans : 2 * trans, cols] = sine
    big[1].wait()
    big[2].wait()
    norms = [None, None]
    scores = [None, None]
    for step in range(blocks):
        col0 = step * chunk
        part0 = step * tiles * part_dev * 2
        refs0 = step * tiles * ori_dev * 2
        split_planes((part_dev, tiles, lambda i, t: part_ref[i, :, pl.ds(col0 + t * lanes, lanes)]), part_rows, part0)
        split_planes((ori_dev, tiles, lambda j, t: refs_ref[j, :, pl.ds(col0 + t * lanes, lanes)]), refs_rows, refs0)
        squares = []
        weighted = [[], []]
        for t in range(tiles):
            cols = slice(col0 + t * lanes, col0 + (t + 1) * lanes)
            part_r = read_plane(part_rows, part0, part_dev, t, 0)
            part_m = read_plane(part_rows, part0, part_dev, t, 1)
            refs_r = read_plane(refs_rows, refs0, ori_dev, t, 0)
            refs_m = read_plane(refs_rows, refs0, ori_dev, t, 1)
            ctf = pix_ref[0:n, cols]
            scaled_ref[0:n, cols] = part_r * ctf
            scaled_ref[n : 2 * n, cols] = part_m * ctf
            inv = jnp.concatenate([pix_ref[n : n + 8, cols]] * (ori_dev // 8), axis=0)
            for p, plane in enumerate((refs_r, refs_m)):
                weighted[p].append((plane * inv).astype(bf16))
                planes_ref[:, pl.ds(2 * col0 + p * chunk + t * lanes, lanes)] = plane.astype(bf16)
            power = jnp.concatenate([refs_r * refs_r + refs_m * refs_m, part_r * part_r + part_m * part_m], axis=0)
            high = power.astype(bf16).astype(f32)
            squares.append((high.astype(bf16), (power - high).astype(bf16)))
        for t in range(tiles):
            cols = slice(col0 + t * lanes, col0 + (t + 1) * lanes)

            def store(p, i, value):
                at = 2 * col0 + p * chunk + t * lanes
                img_ref[i * trans : (i + 1) * trans, at : at + lanes] = value

            write_images(
                store, scaled_ref, col0 + t * lanes, wave_ref[0:trans, cols], wave_ref[trans : 2 * trans, cols], n
            )
        at = 2 * col0
        more = nt(img_ref[:, at : at + chunk], jnp.concatenate(weighted[0], axis=1)) + nt(
            img_ref[:, at + chunk : at + 2 * chunk], jnp.concatenate(weighted[1], axis=1)
        )
        scores[0] = more if scores[0] is None else scores[0] + more
        for p in range(2):
            more = nt(jnp.concatenate([sq[p] for sq in squares], axis=1), hot_ref[:, col0 : col0 + chunk])
            norms[p] = more if norms[p] is None else norms[p] + more
    scores = scores[0]

    both = ori_dev + part_dev
    norms = norms[0] + norms[1]
    ref_norm = norms[0:ori_dev]
    part_norm = norms[ori_dev:both]
    ctf_square = ctf_rows * ctf_rows
    energy = ref_norm / sigma
    quadratic = 0.5 * nt(ctf_square, energy, precision=highest)
    allowed = jnp.where(mask_ref[...] == 1, 1.0, 0.0)
    wide = (part_dev, trans, ori_dev)
    scores = scores.reshape(wide) - jnp.broadcast_to(quadratic[:, None, :], wide)
    scores = jnp.where(jnp.broadcast_to(allowed[:, None, :], wide) > 0.5, scores, -1e30)
    peak = jnp.max(jnp.max(scores, axis=1, keepdims=True), axis=2, keepdims=True)
    e = jnp.exp(scores - peak)
    orient_sums = jnp.sum(e, axis=1)
    e_wide = e.reshape(pairs, ori_dev)
    e_ref[...] = e_wide
    high = e_wide.astype(bf16)
    e_rows = jnp.concatenate([high.astype(f32), e_wide - high.astype(f32)], axis=1).astype(bf16)

    cross = None
    for step in range(blocks):
        col0 = step * chunk
        plane = planes_ref[:, 2 * col0 : 2 * (col0 + chunk)]
        mixed = nn(e_rows, jnp.concatenate([plane, plane], axis=0))
        total = None
        for p in range(2):
            at = 2 * col0 + p * chunk
            part = mixed[:, p * chunk : (p + 1) * chunk] * img_ref[:, at : at + chunk].astype(f32)
            total = part if total is None else total + part
        folded = total.reshape(part_dev, trans // 8, 8, chunk).sum(axis=1).reshape(part_dev * 8, chunk)
        folded = folded.astype(bf16)
        more = [
            nt(folded[:, k * chunk // 2 : (k + 1) * chunk // 2], hot_ref[:, col0 + k * chunk // 2 : col0 + (k + 1) * chunk // 2])
            for k in range(2)
        ]
        cross = more if cross is None else [old + new for old, new in zip(cross, more)]
    cross = (cross[0] + cross[1]).reshape(part_dev, 8, shells).sum(axis=1)
    total = jnp.sum(orient_sums, axis=1, keepdims=True)
    third = ctf_square * nn(orient_sums, ref_norm, precision=highest)
    noise = part_norm * total - 2.0 * cross + third
    lane = lax.broadcasted_iota(jnp.int32, (part_dev, lanes), 1)
    stat = jnp.concatenate([noise, jnp.zeros((part_dev, lanes - shells), f32)], axis=1)
    for k, piece in enumerate(pieces(peak.reshape(part_dev, 1), 3) + pieces(total, 3)):
        stat = jnp.where(lane == shells + k, jnp.broadcast_to(piece.astype(f32), lane.shape), stat)
    message = jnp.concatenate([e_wide.T, stat], axis=0).astype(bf16)

    def spread(dest, carry):
        message_ref[dest] = message
        return carry

    lax.fori_loop(0, message_ref.shape[0], spread, 0, unroll=8)


def column_kernel(
    group_hbm,
    recv_ref,
    phase_hbm,
    shell_hbm,
    table_hbm,
    scaled_ref,
    wave_ref,
    square_hbm,
    group_ref,
    phase_ref,
    shell_ref,
    table_ref,
    square_ref,
    rows_ref,
    planes_ref,
    ctf_ref,
    sems,
):
    sources, part_dev, _, width = recv_ref.shape
    trans = phase_ref.shape[0]
    shells = table_ref.shape[1]
    pairs = part_dev * trans
    tiles = width // lanes
    span = wave_tile // lanes
    start = pl.multiple_of(lax.axis_index("dom") * width, width)
    copies = start_all(
        [
            (group_hbm, group_ref),
            (table_hbm, table_ref),
            (shell_hbm.at[:, pl.ds(start, width)], shell_ref),
            (phase_hbm.at[:, pl.ds(start, width)], phase_ref),
        ],
        sems,
    )
    for copy in copies:
        copy.wait()
    for i in range(sources * part_dev):
        rows_ref[pl.ds(i, 1), :] = table_ref[pl.ds(group_ref[i], 1), :]
    hot = one_hot(shell_ref[...], shells)
    everyone = rows_ref[...]
    ctf_ref[...] = sum(nn(piece, hot) for piece in pieces(everyone, 3))
    for t in range(tiles):
        at = (t // span * 2 * span + t % span) * lanes
        sine, cosine = sin_cos(phase_ref[:, pl.ds(t * lanes, lanes)])
        for wave, offset in ((cosine, at), (sine, at + wave_tile)):
            high = wave.astype(bf16)
            wave_ref[0:trans, pl.ds(offset, lanes)] = high
            wave_ref[trans : 2 * trans, pl.ds(offset, lanes)] = (wave - high.astype(f32)).astype(bf16)
    square = everyone * everyone
    high = square.astype(bf16).astype(f32)
    squares = jnp.concatenate([high, square - high], axis=1)
    square_ref[...] = (
        jnp.broadcast_to(squares[:, None, :], (sources * part_dev, trans, 2 * shells))
        .reshape(sources * pairs, 2 * shells)
        .astype(bf16)
    )
    square_copy = pltpu.make_async_copy(square_ref, square_hbm, sems.at[0])
    square_copy.start()
    n = part_dev

    def source_step(src, carry):
        plane0 = pl.multiple_of(src * (tiles * part_dev * 2), tiles * part_dev * 2)
        split_planes((part_dev, tiles, lambda i, t: recv_ref[src, i, :, pl.ds(t * lanes, lanes)]), planes_ref, plane0)
        rows = pl.ds(pl.multiple_of(src * n, n), n)
        for t in range(tiles):
            cols = pl.ds(t * lanes, lanes)
            ctf = ctf_ref[rows, cols]
            for p in range(2):
                scaled_ref[p, rows, cols] = read_plane(planes_ref, plane0, part_dev, t, p) * ctf
        return carry

    lax.fori_loop(0, sources, source_step, 0, unroll=2)
    square_copy.wait()


def sum_kernel(
    orients,
    shells,
    scale,
    scaled_ref,
    wave_ref,
    square_hbm,
    recv_ref,
    e_ref,
    post_ref,
    sums_ref,
    weights_ref,
    noise_ref,
    square_ref,
    half_ref,
    left_ref,
    share_ref,
    sem,
):
    pairs, ori_dev = e_ref.shape
    part_dev = recv_ref.shape[1] - ori_dev
    trans = pairs // part_dev
    sources = recv_ref.shape[0] // orients
    square_copy = pltpu.make_async_copy(square_hbm, square_ref, sem)
    square_copy.start()
    me = lax.axis_index("dom")
    mine = lax.axis_index("orient")
    lane_part = lax.broadcasted_iota(jnp.int32, (part_dev, pairs), 1) // trans
    own = lane_part == lax.broadcasted_iota(jnp.int32, (part_dev, pairs), 0)
    lane = lax.broadcasted_iota(jnp.int32, (ori_dev, pairs), 1)
    lower = lane < pairs // 2
    half_part = lane % (pairs // 2) // trans
    row = lax.broadcasted_iota(jnp.int32, (lanes, 2 * lanes), 0) - shells
    upper = lax.broadcasted_iota(jnp.int32, (lanes, 2 * lanes), 1) // lanes
    picker = jnp.where((row >= 3 * upper) & (row < 3 * upper + 3), 1.0, 0.0).astype(bf16)

    stats = recv_ref[:, ori_dev : ori_dev + part_dev, :].astype(f32)
    rows = stats.reshape(sources * orients * part_dev, lanes).astype(bf16)
    decoded = nn(rows, picker)
    shape = (sources, orients, part_dev, lanes)
    peaks = decoded[:, 0:lanes].reshape(shape)
    totals = decoded[:, lanes : 2 * lanes].reshape(shape)
    shares = jnp.exp(peaks - jnp.max(peaks, axis=1, keepdims=True))
    shares = shares * (1.0 / jnp.sum(shares * totals, axis=1, keepdims=True))
    noise = jnp.sum(shares * stats.reshape(shape), axis=(0, 1))
    noise_ref[...] = jnp.sum(noise, axis=0, keepdims=True)[:, 0:shells] * scale
    share_ref[...] = shares.reshape(sources * orients, part_dev, lanes)
    for src in range(sources):
        factor = share_ref[src * orients + mine]
        lane = jnp.sum(jnp.where(own, factor, 0.0), axis=0, keepdims=True)
        post = recv_ref[src * orients + mine, 0:ori_dev, :].astype(f32) * lane
        high = post.astype(bf16).astype(f32)
        low = post - high
        half_ref[:, pl.ds(src * pairs, pairs)] = jnp.concatenate([high, low], axis=0).astype(bf16)
        turned = [pltpu.roll(x, pairs // 2, 1) for x in (high, low)]
        mixes = (jnp.where(lower, high, turned[1]), jnp.where(lower, turned[0], low))
        highs = (high, turned[0])
        for i in range(part_dev):
            rows = pl.ds((src * part_dev + i) * ori_dev, ori_dev)
            group = i // (part_dev // 2)
            here = half_part == i % (part_dev // 2)
            left_ref[rows, 0:pairs] = jnp.where(here, mixes[group], 0.0).astype(bf16)
            left_ref[rows, pairs : 2 * pairs] = jnp.where(here & lower, highs[group], 0.0).astype(bf16)
    factor = share_ref[me * orients + mine][:, 0:ori_dev]
    wide = (part_dev, trans, ori_dev)
    post_ref[...] = (e_ref[...].reshape(wide) * jnp.broadcast_to(factor[:, None, :], wide)).reshape(pairs, ori_dev)
    for tile in range(sums_ref.shape[2] // wave_tile):
        cols = slice(tile * wave_tile, (tile + 1) * wave_tile)
        waves = wave_ref[:, 2 * tile * wave_tile : 2 * (tile + 1) * wave_tile]
        high = waves[0:trans]
        low = waves[trans : 2 * trans]
        mixed = nn(left_ref[...], jnp.concatenate([high] * part_dev + [low] * part_dev, axis=0))
        sums = [None, None]
        for i in range(sources * part_dev):
            block = mixed[i * ori_dev : (i + 1) * ori_dev]
            cosine = block[:, 0:wave_tile]
            sine = block[:, wave_tile : 2 * wave_tile]
            r = jnp.broadcast_to(scaled_ref[0, i : i + 1, cols], cosine.shape)
            m = jnp.broadcast_to(scaled_ref[1, i : i + 1, cols], cosine.shape)
            more = (r * cosine - m * sine, r * sine + m * cosine)
            sums = [new if old is None else old + new for old, new in zip(sums, more)]
        for p in range(2):
            for j in range(ori_dev):
                sums_ref[j, p : p + 1, cols] = sums[p][j : j + 1, :]
    square_copy.wait()
    weights = nn(half_ref[...], square_ref[...])
    weights = weights[0:ori_dev] + weights[ori_dev : 2 * ori_dev]
    weights_ref[...] = weights[:, 0:shells] + weights[:, shells : 2 * shells]


def on_device(particles, references, phases, mask, ctf_group, ctf_table, shell_index, sigma2):
    part_dev, _, pixels = particles.shape
    ori_dev = references.shape[0]
    trans = phases.shape[0]
    shells = ctf_table.shape[1]
    dom = lax.axis_size("dom")
    orients = lax.axis_size("orient")
    width = pixels // dom
    pairs = part_dev * trans
    chunk = 4096
    shell_row = shell_index.reshape(1, pixels)
    sigma_row = sigma2.reshape(1, shells)
    vmem = pl.BlockSpec(memory_space=pltpu.VMEM)
    smem = pl.BlockSpec(memory_space=pltpu.SMEM)
    anywhere = pl.BlockSpec(memory_space=pl.ANY)
    params = pltpu.CompilerParams(vmem_limit_bytes=20 * 1024 * 1024)
    far = lambda x: pltpu.with_memory_space_constraint(x, pltpu.HBM)
    dma = pltpu.SemaphoreType.DMA

    send = pl.pallas_call(
        pack_kernel,
        out_shape=pltpu.VMEM((dom, part_dev, 2, width), bf16),
        in_specs=[anywhere],
        out_specs=vmem,
        scratch_shapes=[dma((dom,))],
        compiler_params=params,
        name="pack",
    )(far(particles))
    recv = lax.all_to_all(send, "dom", 0, 0)

    both = ori_dev + part_dev
    message, e = pl.pallas_call(
        functools.partial(score_kernel, chunk),
        out_shape=(
            pltpu.VMEM((dom * orients, both, lanes), bf16),
            jax.ShapeDtypeStruct((pairs, ori_dev), f32),
        ),
        in_specs=[anywhere] * 8,
        out_specs=(vmem, vmem),
        scratch_shapes=[
            pltpu.VMEM(particles.shape, bf16),
            pltpu.VMEM(references.shape, bf16),
            pltpu.VMEM(phases.shape, f32),
            pltpu.VMEM((1, pixels), jnp.int32),
            pltpu.VMEM(mask.shape, jnp.int32),
            pltpu.VMEM(ctf_table.shape, f32),
            pltpu.VMEM((1, shells), f32),
            pltpu.SMEM(ctf_group.shape, jnp.int32),
            pltpu.VMEM((pixels // lanes * part_dev * 2 + 8, lanes), f32),
            pltpu.VMEM((pixels // lanes * ori_dev * 2 + 8, lanes), f32),
            pltpu.VMEM((pairs, 2 * pixels), bf16),
            pltpu.VMEM((ori_dev, 2 * pixels), bf16),
            pltpu.VMEM((shells, pixels), bf16),
            pltpu.VMEM((2 * part_dev, pixels), f32),
            pltpu.VMEM((part_dev + 8, pixels), f32),
            pltpu.VMEM((2 * trans, pixels), f32),
            pltpu.VMEM((part_dev, shells), f32),
            dma((5,)),
            dma((3,)),
        ],
        compiler_params=params,
        name="scores",
    )(
        far(ctf_group),
        far(particles),
        far(references),
        far(phases),
        far(shell_row),
        far(mask),
        far(ctf_table),
        far(sigma_row),
    )

    messages = lax.all_to_all(message, ("dom", "orient"), 0, 0)

    particles_all = dom * part_dev
    columns = (
        ((2, particles_all, width), f32),
        ((2 * trans, 2 * width), bf16),
        ((particles_all * trans, 2 * shells), bf16),
    )
    scaled, waves, squares = pl.pallas_call(
        column_kernel,
        out_shape=(pltpu.VMEM(*columns[0]), pltpu.VMEM(*columns[1]), pltpu.HBM(*columns[2])),
        in_specs=[anywhere, vmem] + [anywhere] * 3,
        out_specs=(vmem, vmem, anywhere),
        scratch_shapes=[
            pltpu.SMEM(ctf_group.shape, jnp.int32),
            pltpu.VMEM((trans, width), f32),
            pltpu.VMEM((1, width), jnp.int32),
            pltpu.VMEM(ctf_table.shape, f32),
        ]
        + [
            pltpu.VMEM(*columns[2]),
            pltpu.VMEM((particles_all, shells), f32),
            pltpu.VMEM((particles_all * 2 * width // lanes + 8, lanes), f32),
            pltpu.VMEM((particles_all, width), f32),
            dma((4,)),
        ],
        compiler_params=params,
        name="columns",
    )(far(ctf_group), recv, far(phases), far(shell_row), far(ctf_table))

    scale = shells / (part_dev * dom * pixels)
    posterior, image_sums, ctf_weights, noise = pl.pallas_call(
        functools.partial(sum_kernel, orients, shells, scale),
        out_shape=(
            jax.ShapeDtypeStruct((pairs, ori_dev), f32),
            jax.ShapeDtypeStruct((ori_dev, 2, width), f32),
            jax.ShapeDtypeStruct((ori_dev, shells), f32),
            jax.ShapeDtypeStruct((1, shells), f32),
        ),
        in_specs=[vmem, vmem, anywhere, vmem, vmem],
        out_specs=(vmem, vmem, vmem, vmem),
        scratch_shapes=[
            pltpu.VMEM(*columns[2]),
            pltpu.VMEM((2 * ori_dev, particles_all * trans), bf16),
            pltpu.VMEM((particles_all * ori_dev, 2 * pairs), bf16),
            pltpu.VMEM((dom * orients, part_dev, lanes), f32),
            dma,
        ],
        compiler_params=params,
        name="sums",
    )(scaled, waves, far(squares), messages, e)
    return (
        posterior.reshape(part_dev, trans, ori_dev),
        image_sums,
        ctf_weights,
        noise.reshape(shells),
    )


def solution(mesh):
    return jax.shard_map(
        on_device,
        mesh=mesh,
        in_specs=(
            P("dom", None, None),
            P("orient", None, None),
            P(),
            P("dom", "orient"),
            P(),
            P(),
            P(),
            P(),
        ),
        out_specs=(P("dom", None, "orient"), P("orient", None, "dom"), P("orient", None), P()),
        check_vma=False,
    )
```
